32 devices in a mesh: panel: 16 (over z, y, core), rep: 2 (over x).
Axes of the slice: x: 2, y: 2, z: 4, core: 2. Of those that a mesh axis runs over, the one named last changes fastest.
Arguments:
- x_src: bfloat16 [2048, 128], P('panel'), may hold values from -6 to 6
- x_dst: bfloat16 [16384, 128], P(('panel', 'rep')), may hold values from -6 to 6
- weight: bfloat16 [128, 512], replicated, may hold values from -0.5 to 0.5
- att_src: float32 [8, 64], replicated, may hold values from -0.75 to 0.75
- att_dst: float32 [8, 64], replicated, may hold values from -0.75 to 0.75
- grad_out: bfloat16 [16384, 512], P(('panel', 'rep')), may hold values from -6 to 6
- block_rows: int32 [512], P(('panel', 'rep')), may hold values from 0 to 3, as said below
- block_cols: int32 [512], P(('panel', 'rep')), may hold values from 0 to 15
- block_masks: int32 [512, 128, 128], P(('panel', 'rep')), may hold values from 0 to 1, as said below
- block_counts: int32 [32], P(('panel', 'rep')), may hold values from 2 to 16, as said below
Outputs:
- grad_src: float32 [2048, 128], P('panel')
- grad_dst: float32 [16384, 128], P(('panel', 'rep'))
- grad_weight: float32 [128, 512], replicated
- grad_att_src: float32 [8, 64], replicated
- grad_att_dst: float32 [8, 64], replicated
The draws below stay inside these ranges and needn't reach their ends.
Inputs may be any that keep to these rules, and one draw needn't show every extreme that they name: `block_counts`: live block slots of one device; at least one device has exactly 16. The pairs of block_rows and block_cols within one device's 16 slots are distinct. `block_masks`: slots at or after a device's count of live blocks hold only zeros.
All inputs are finite; a program needn't handle non-finite values.
Results may differ from the reference program's by a relative error of at most 0.012.
The reference program's roundings to bfloat16 on the way (of `proj_src` and `proj_dst`) count: a program that leaves them out, or rounds other values in their place, can miss the bound.
Values may be sent and summed in bfloat16 or wider, within the bound.
A program may use at most 128 MiB of HBM per device.

```python
import jax
import jax.numpy as jnp
from jax import lax

HEADS = 8
HEAD_DIM = 64
IN = 128
WIDTH = 512
BLK = 128
DST_DEV = 512
NB_DEV = 16
NSRC = 2048
NDST = 16384
N_PANEL = 16
N_REP = 2


def block_layout(key):
    device_count = N_PANEL * N_REP
    dest_blocks = DST_DEV // BLK
    source_blocks = NSRC // BLK
    keys_all = jax.random.split(jax.random.fold_in(key, 17), 5)
    halvings = jax.random.randint(keys_all[0], (device_count,), 0, 4)
    fullest = jax.random.randint(keys_all[1], (), 0, device_count)
    halvings = jnp.where(jnp.arange(device_count) == fullest, 0, halvings).astype(jnp.int32)
    live_counts = jnp.right_shift(jnp.full((device_count,), NB_DEV, jnp.int32), halvings)
    pair_keys = jax.random.split(keys_all[2], device_count)

    def pick_pairs(one_key):
        return jax.random.permutation(one_key, dest_blocks * source_blocks)[:NB_DEV]
    pair_codes = jax.vmap(pick_pairs)(pair_keys).astype(jnp.int32)
    rows_drawn = (pair_codes // source_blocks).reshape(-1).astype(jnp.int32)
    cols_drawn = (pair_codes % source_blocks).reshape(-1).astype(jnp.int32)
    density = jax.random.randint(keys_all[3], (device_count, NB_DEV, 1, 1), 64, 512)
    edge_bits = jax.random.randint(keys_all[4], (device_count, NB_DEV, BLK, BLK), 0, 1024) < density
    live_slots = (jnp.arange(NB_DEV)[None, :] < live_counts[:, None])[:, :, None, None]
    masks_drawn = jnp.where(edge_bits & live_slots, 1, 0).astype(jnp.int32).reshape(device_count * NB_DEV, BLK, BLK)
    return (live_counts, rows_drawn, cols_drawn, masks_drawn)


def draw_block_counts(key, part):
    return block_layout(key)[0]


def draw_block_rows(key, part):
    return block_layout(key)[1]


def draw_block_cols(key, part):
    return block_layout(key)[2]


def draw_block_masks(key, part):
    return block_layout(key)[3]


def level_of(key, dims, pieces, least, high):
    level, own = 1.0, jax.random.fold_in(key, 6)
    for dim, parts in pieces:
        draws = jnp.exp(jax.random.uniform(jax.random.fold_in(own, dim), (parts,), jnp.float32, least / len(pieces), high / len(pieces)))
        level = level * jnp.repeat(draws, dims[dim] // parts).reshape([-1 if axis == dim else 1 for axis in range(len(dims))])
    return level


def scatter_about(rng, extent, width, limit, shards=(), kind=jnp.bfloat16):
    array = width * jax.random.normal(rng, extent, jnp.float32)
    if shards:
        array = array * level_of(rng, extent, shards, -0.22, 0.18)
    return jnp.clip(array, -limit, limit).astype(kind)


def setup_inputs(seed: int = 0) -> dict:
    arg_keys = jax.random.split(jax.random.key(seed), 11)
    return {
        "x_src": scatter_about(arg_keys[0], (NSRC, IN), 1.0, 6.0, ((0, 16),)),
        "x_dst": scatter_about(arg_keys[1], (NDST, IN), 1.0, 6.0, ((0, 32),)),
        "weight": scatter_about(arg_keys[2], (IN, WIDTH), IN ** -0.5, 0.5),
        "att_src": scatter_about(arg_keys[3], (HEADS, HEAD_DIM), HEAD_DIM ** -0.5, 0.75, (), jnp.float32),
        "att_dst": scatter_about(arg_keys[4], (HEADS, HEAD_DIM), HEAD_DIM ** -0.5, 0.75, (), jnp.float32),
        "grad_out": scatter_about(arg_keys[5], (NDST, WIDTH), 1.0, 6.0, ((0, 32),)),
        "block_rows": draw_block_rows(jax.random.fold_in(arg_keys[10], 71), 0),
        "block_cols": draw_block_cols(jax.random.fold_in(arg_keys[10], 71), 0),
        "block_masks": draw_block_masks(jax.random.fold_in(arg_keys[10], 71), 0),
        "block_counts": draw_block_counts(jax.random.fold_in(arg_keys[10], 71), 0),
    }


HIGHEST_PRECISION = lax.Precision.HIGHEST


def smooth_leaky(values):
    return 0.2 * values + 0.8 * jax.nn.softplus(values)


def smooth_slope(values):
    return 0.2 + 0.8 * jax.nn.sigmoid(values)


def to_bfloat(values):
    return lax.optimization_barrier(values.astype(jnp.bfloat16)).astype(jnp.float32)


def add_slice(target, update, start, axis):
    current = lax.dynamic_slice_in_dim(target, start, update.shape[axis], axis)
    return lax.dynamic_update_slice_in_dim(target, current + update, start, axis)


def reference(x_src, x_dst, weight, att_src, att_dst, grad_out, block_rows, block_cols, block_masks, block_counts):
    device_count = N_PANEL * N_REP
    proj_src = jnp.dot(x_src, weight, preferred_element_type=jnp.float32).astype(jnp.bfloat16)
    source_feats = proj_src.astype(jnp.float32).reshape(NSRC, HEADS, HEAD_DIM)
    score_src = jnp.einsum("jhk,hk->hj", source_feats, att_src, precision=HIGHEST_PRECISION)
    proj_dst = jnp.dot(x_dst, weight, preferred_element_type=jnp.float32).astype(jnp.bfloat16)
    dest_feats = proj_dst.astype(jnp.float32).reshape(NDST, HEADS, HEAD_DIM)
    score_dst = jnp.einsum("ihk,hk->hi", dest_feats, att_dst, precision=HIGHEST_PRECISION)
    score_self = jnp.einsum("ihk,hk->hi", dest_feats, att_src, precision=HIGHEST_PRECISION)
    cotangent = grad_out.astype(jnp.float32).reshape(NDST, HEADS, HEAD_DIM)
    rows_all = block_rows.reshape(device_count, NB_DEV)
    cols_all = block_cols.reshape(device_count, NB_DEV)
    masks_all = block_masks.reshape(device_count, NB_DEV, BLK, BLK)

    def device_step(carried, device):
        grad_source, grad_score_src = carried
        row_start = device * DST_DEV
        feats = lax.dynamic_slice_in_dim(dest_feats, row_start, DST_DEV, 0)
        cotan = lax.dynamic_slice_in_dim(cotangent, row_start, DST_DEV, 0)
        score_d = lax.dynamic_slice_in_dim(score_dst, row_start, DST_DEV, 1)
        score_own = lax.dynamic_slice_in_dim(score_self, row_start, DST_DEV, 1)
        dest_index = rows_all[device]
        source_index = cols_all[device]
        masks = masks_all[device]
        live_count = block_counts[device]

        def block_scores(block_index):
            dest_block = dest_index[block_index] * BLK
            source_block = source_index[block_index] * BLK
            pre_score = (lax.dynamic_slice_in_dim(score_d, dest_block, BLK, 1)[:, :, None]
                         + lax.dynamic_slice_in_dim(score_src, source_block, BLK, 1)[:, None, :])
            edge_weight = jnp.exp(smooth_leaky(pre_score)) * masks[block_index].astype(jnp.float32)[None]
            source_rows = lax.dynamic_slice_in_dim(source_feats, source_block, BLK, 0)
            return dest_block, source_block, pre_score, edge_weight, source_rows

        def forward_block(block_index, carried_fwd):
            denominator, numerator = carried_fwd
            dest_block, source_block, pre_score, edge_weight, source_rows = block_scores(block_index)
            part_num = jnp.einsum("hij,jhk->ihk", to_bfloat(edge_weight), source_rows, precision=HIGHEST_PRECISION)
            denominator = add_slice(denominator, edge_weight.sum(axis=2), dest_block, 1)
            numerator = add_slice(numerator, part_num, dest_block, 0)
            return denominator, numerator

        zero_start = jnp.int32(0)
        denominator, numerator = lax.fori_loop(zero_start, live_count, forward_block,
                                               (jnp.zeros((HEADS, DST_DEV), jnp.float32),
                                                jnp.zeros((DST_DEV, HEADS, HEAD_DIM), jnp.float32)))
        pre_self = score_d + score_own
        self_weight = jnp.exp(smooth_leaky(pre_self))
        denominator = denominator + self_weight
        numerator = numerator + self_weight.T[:, :, None] * feats
        attended = numerator / denominator.T[:, :, None]
        centred = jnp.sum(cotan * attended, axis=2).T

        def backward_block(block_index, carried_bwd):
            grad_source, grad_score_src, grad_score_dst = carried_bwd
            dest_block, source_block, pre_score, edge_weight, source_rows = block_scores(block_index)
            attention = edge_weight / lax.dynamic_slice_in_dim(denominator, dest_block, BLK, 1)[:, :, None]
            cotan_rows = lax.dynamic_slice_in_dim(cotan, dest_block, BLK, 0)
            pair_grad = jnp.einsum("ihk,jhk->hij", cotan_rows, source_rows, precision=HIGHEST_PRECISION)
            centred_rows = lax.dynamic_slice_in_dim(centred, dest_block, BLK, 1)
            score_grad = attention * (pair_grad - centred_rows[:, :, None]) * smooth_slope(pre_score)
            feat_grad = jnp.einsum("hij,ihk->jhk", to_bfloat(attention), cotan_rows, precision=HIGHEST_PRECISION)
            grad_source = add_slice(grad_source, feat_grad, source_block, 0)
            grad_score_src = add_slice(grad_score_src, score_grad.sum(axis=1), source_block, 1)
            grad_score_dst = add_slice(grad_score_dst, score_grad.sum(axis=2), dest_block, 1)
            return grad_source, grad_score_src, grad_score_dst

        grad_source, grad_score_src, grad_score_dst = lax.fori_loop(
            zero_start, live_count, backward_block,
            (grad_source, grad_score_src, jnp.zeros((HEADS, DST_DEV), jnp.float32)))
        self_attention = self_weight / denominator
        self_pair = jnp.sum(cotan * feats, axis=2).T
        self_grad = self_attention * (self_pair - centred) * smooth_slope(pre_self)
        grad_score_dst = grad_score_dst + self_grad
        grad_dest = (self_attention.T[:, :, None] * cotan + self_grad.T[:, :, None] * att_src[None]
                     + grad_score_dst.T[:, :, None] * att_dst[None])
        att_self = jnp.einsum("hi,ihk->hk", self_grad, feats, precision=HIGHEST_PRECISION)
        att_dest = jnp.einsum("hi,ihk->hk", grad_score_dst, feats, precision=HIGHEST_PRECISION)
        return (grad_source, grad_score_src), (grad_dest, att_self, att_dest)

    initial = (jnp.zeros((NSRC, HEADS, HEAD_DIM), jnp.float32), jnp.zeros((HEADS, NSRC), jnp.float32))
    (grad_source, grad_score_src), (grad_dest, att_self, att_dest) = lax.scan(
        device_step, initial, jnp.arange(device_count, dtype=jnp.int32))
    grad_source = grad_source + grad_score_src.T[:, :, None] * att_src[None]
    grad_att_src = jnp.einsum("hj,jhk->hk", grad_score_src, source_feats, precision=HIGHEST_PRECISION) + att_self.sum(axis=0)
    grad_att_dst = att_dest.sum(axis=0)
    source_flat = grad_source.reshape(NSRC, WIDTH)
    dest_flat = grad_dest.reshape(NDST, WIDTH)
    weight_t = weight.astype(jnp.float32).T
    grad_src = jnp.dot(source_flat, weight_t, precision=HIGHEST_PRECISION)
    grad_dst = jnp.dot(dest_flat, weight_t, precision=HIGHEST_PRECISION)
    grad_weight = (jnp.dot(x_src.astype(jnp.float32).T, source_flat, precision=HIGHEST_PRECISION)
                   + jnp.dot(x_dst.astype(jnp.float32).T, dest_flat, precision=HIGHEST_PRECISION))
    return grad_src, grad_dst, grad_weight, grad_att_src, grad_att_dst
```

```python
import jax
import jax.numpy as jnp
from jax import lax
from jax.experimental import pallas as pl
from jax.experimental.pallas import tpu as pltpu
from jax.sharding import PartitionSpec as P

F32 = jnp.float32
BF16 = jnp.bfloat16
MESH = pl.DeviceIdType.MESH
LANES = 128


def mm(a, b, ca=1, cb=0):
    return lax.dot_general(a, b, (((ca,), (cb,)), ((), ())), preferred_element_type=F32)


def split(values, parts):
    pieces = []
    for _ in range(parts):
        piece = values.astype(BF16)
        pieces.append(piece)
        values = values - piece.astype(F32)
    return pieces


def mm_split(a, b, parts, ca=1, cb=0):
    return sum(mm(piece, b, ca, cb) for piece in split(a, parts))


def edge_terms(pre):
    small = jnp.exp(-jnp.abs(pre))
    grown = 1.0 + small
    inverse = 1.0 / grown
    sigma = 0.2 * pre + 0.8 * (jnp.maximum(pre, 0.0) + jnp.log(grown))
    sigmoid = jnp.where(pre >= 0.0, inverse, small * inverse)
    return jnp.exp(sigma), 0.2 + 0.8 * sigmoid


def iota(shape, dim):
    return lax.broadcasted_iota(jnp.int32, shape, dim)


def layer_kernel(
    rows_ref, cols_ref, count_ref, x_all_ref, x_dst_ref, weight_ref, att_src_ref, att_dst_ref,
    grad_ref, masks_ref,
    grad_dst_ref, part_src_ref, part_weight_ref, part_att_ref,
    proj_src, proj_dst, score_src, score_wide, inv_wide, weights, slopes,
    numer, denom, centre, grad_source, grad_score_src, grad_score_dst,
):
    heads, head_dim = att_src_ref.shape
    width = weight_ref.shape[1]
    pairs = width // LANES
    blk = masks_ref.shape[1]
    source_blocks = x_all_ref.shape[0] // blk
    dest = x_dst_ref.shape[0]
    count = count_ref[0]
    inputs = weight_ref.shape[0]

    lane_head = iota((heads, width), 1) // head_dim
    own = lane_head == iota((heads, width), 0)
    spread_src = jnp.where(own, jnp.concatenate([att_src_ref[...]] * heads, axis=1), 0.0)
    spread_dst = jnp.where(own, jnp.concatenate([att_dst_ref[...]] * heads, axis=1), 0.0)
    pad_rows = jnp.zeros((LANES - heads, width), F32)
    ones_heads = jnp.concatenate([jnp.where(own, 1.0, 0.0), pad_rows], axis=0).astype(BF16)
    tall_src = jnp.concatenate([spread_src, pad_rows], axis=0)
    tall_dst = jnp.concatenate([spread_dst, pad_rows], axis=0)

    for s in range(source_blocks):
        at = slice(s * blk, (s + 1) * blk)
        proj_src[at, :] = mm(x_all_ref[at, :], weight_ref[...]).astype(BF16)
    proj_dst[...] = mm(x_dst_ref[...], weight_ref[...]).astype(BF16)
    for s in range(source_blocks):
        at = slice(s * blk, (s + 1) * blk)
        stacked = jnp.concatenate([p.astype(F32) for p in split(spread_src, 3)], axis=0)
        got = mm(stacked.astype(BF16), proj_src[at, :], 1, 1)
        score_src[s] = got[:heads] + got[heads : 2 * heads] + got[2 * heads :]
    score_d = sum(mm(proj_dst[...], p, 1, 1) for p in split(tall_dst, 3))
    pre_self = score_d + sum(mm(proj_dst[...], p, 1, 1) for p in split(tall_src, 3))
    for h in range(heads):
        score_wide[h] = jnp.broadcast_to(score_d[:, h : h + 1], (dest, LANES))

    numer[...] = jnp.zeros_like(numer)
    denom[...] = jnp.zeros_like(denom)
    grad_source[...] = jnp.zeros_like(grad_source)
    grad_score_src[...] = jnp.zeros_like(grad_score_src)
    grad_score_dst[...] = jnp.zeros_like(grad_score_dst)

    low = (iota((1, LANES), 1) < head_dim).astype(F32).astype(BF16)
    high = (iota((1, LANES), 1) >= head_dim).astype(F32).astype(BF16)
    second = iota((2 * blk, LANES), 0) // blk
    lane = iota((2 * blk, LANES), 1)

    def both(values):
        return jnp.concatenate([values * low, values * high], axis=0)

    def pick(g, with_low):
        head = 2 * g + second
        hit = lane == head
        if with_low:
            hit = hit | (lane == head + heads)
        return jnp.where(hit, 1.0, 0.0)

    def forward(b, carry):
        r = pl.ds(pl.multiple_of(rows_ref[b] * blk, blk), blk)
        c = cols_ref[b]
        src = pl.ds(pl.multiple_of(c * blk, blk), blk)
        live = masks_ref[b] > 0
        scores = score_src[c]
        for g in range(pairs):
            at = slice(g * LANES, (g + 1) * LANES)
            found = []
            for h in (2 * g, 2 * g + 1):
                edge, slope = edge_terms(score_wide[h, r, :] + scores[h : h + 1, :])
                edge = jnp.where(live, edge, 0.0)
                weights[b, h] = edge
                slopes[b, h] = slope
                found.append(edge.astype(BF16))
            right = jnp.concatenate(
                [both(proj_src[src, at]), pick(g, False).astype(BF16)], axis=1
            )
            got = mm(jnp.concatenate(found, axis=1), right)
            numer[r, at] += got[:, :LANES]
            denom[r, :] += got[:, LANES:]
        return carry

    lax.fori_loop(0, count, forward, 0)

    feats = proj_dst[...].astype(F32)
    cotan = grad_ref[...].astype(F32)
    self_weight, self_slope = edge_terms(pre_self)
    inverse = 1.0 / (denom[...] + self_weight)
    total = numer[...] + mm_split(self_weight, ones_heads, 2) * feats
    narrow = mm_split(cotan * total, ones_heads, 2, 1, 1) * inverse
    lanes = iota((dest, LANES), 1)
    narrow = jnp.where(lanes < heads, narrow, 0.0)
    top = narrow.astype(BF16).astype(F32)
    centre[...] = (top + pltpu.roll(narrow - top, heads, 1)).astype(BF16)
    self_att = jnp.where(lanes < heads, self_weight * inverse, 0.0)
    self_pair = mm_split(cotan * feats, ones_heads, 2, 1, 1)
    self_grad = self_att * (self_pair - narrow) * self_slope
    for h in range(heads):
        inv_wide[h] = jnp.broadcast_to(inverse[:, h : h + 1], (dest, LANES))

    def backward(b, carry):
        r = pl.ds(pl.multiple_of(rows_ref[b] * blk, blk), blk)
        c = cols_ref[b]
        src = pl.ds(pl.multiple_of(c * blk, blk), blk)
        for g in range(pairs):
            at = slice(g * LANES, (g + 1) * LANES)
            cot = grad_ref[r, at]
            left = jnp.concatenate([cot, centre[r, :]], axis=1)
            right = jnp.concatenate(
                [both(proj_src[src, at]), (-pick(g, True)).astype(BF16)], axis=1
            )
            apart = mm(left, right, 1, 1)
            shares, grads, sums = [], [], []
            for q in range(2):
                h = 2 * g + q
                share = weights[b, h] * inv_wide[h, r, :]
                grad = share * apart[:, q * blk : (q + 1) * blk] * slopes[b, h]
                sums.append(jnp.sum(grad, axis=0, keepdims=True))
                shares.append(share.astype(BF16))
                grads.append(grad.astype(BF16))
            grad_score_src[c, 2 * g : 2 * g + 2, :] += jnp.concatenate(sums, axis=0)
            grad_score_dst[r, :] += mm(
                jnp.concatenate(grads, axis=1), pick(g, False).astype(BF16)
            )
            grad_source[src, at] += mm(jnp.concatenate(shares, axis=0), both(cot), 0, 0)
        return carry

    lax.fori_loop(0, count, backward, 0)

    score_grad = grad_score_dst[...] + self_grad
    self_grad_b = self_grad.astype(BF16)
    score_grad_b = score_grad.astype(BF16)
    flat = (
        mm_split(self_att, ones_heads, 2) * cotan
        + mm(self_grad_b, tall_src.astype(BF16))
        + mm(score_grad_b, tall_dst.astype(BF16))
    ).astype(BF16)
    grad_dst_ref[...] = mm(flat, weight_ref[...], 1, 1)
    part_weight = mm(x_dst_ref[...], flat, 0, 0)
    att_src_part = mm(self_grad_b, proj_dst[...], 0, 0)[:heads]
    att_dst_part = mm(score_grad_b, proj_dst[...], 0, 0)[:heads]

    spread_b = spread_src.astype(BF16)
    for s in range(source_blocks):
        at = slice(s * blk, (s + 1) * blk)
        scores = grad_score_src[s].astype(BF16)
        source = (grad_source[at, :] + mm(scores, spread_b, 0, 0)).astype(BF16)
        part_src_ref[at, :] = mm(source, weight_ref[...], 1, 1).astype(part_src_ref.dtype)
        part_weight += mm(x_all_ref[at, :], source, 0, 0)
        att_src_part += mm(scores, proj_src[at, :])
    for g in range(pairs):
        part_weight_ref[g * inputs : (g + 1) * inputs, :] = part_weight[
            :, g * LANES : (g + 1) * LANES
        ].astype(part_weight_ref.dtype)
    src_row = jnp.sum(jnp.where(own, att_src_part, 0.0), axis=0, keepdims=True)
    dst_row = jnp.sum(jnp.where(own, att_dst_part, 0.0), axis=0, keepdims=True)
    stack = [row[:, g * LANES : (g + 1) * LANES] for row in (src_row, dst_row) for g in range(pairs)]
    att = jnp.concatenate(stack, axis=0)
    part_att_ref[...] = jnp.concatenate(
        [att.astype(BF16).astype(F32), att - att.astype(BF16).astype(F32)], axis=0
    ).astype(part_att_ref.dtype)


def layer(x_all, x_dst, weight, att_src, att_dst, grad_out, rows, cols, masks, counts):
    heads = att_src.shape[0]
    inputs, width = weight.shape
    slots, blk = masks.shape[:2]
    sources, dest = x_all.shape[0], x_dst.shape[0]
    blocks = sources // blk
    vmem = pl.BlockSpec(memory_space=pltpu.VMEM)
    smem = pl.BlockSpec(memory_space=pltpu.SMEM)
    return pl.pallas_call(
        layer_kernel,
        out_shape=(
            jax.ShapeDtypeStruct((dest, inputs), F32),
            jax.ShapeDtypeStruct((sources, inputs), BF16),
            jax.ShapeDtypeStruct((width // LANES * inputs, LANES), BF16),
            jax.ShapeDtypeStruct((16, LANES), BF16),
        ),
        in_specs=[smem] * 3 + [vmem] * 7,
        out_specs=(vmem,) * 4,
        scratch_shapes=[
            pltpu.VMEM((sources, width), BF16),
            pltpu.VMEM((dest, width), BF16),
            pltpu.VMEM((blocks, heads, blk), F32),
            pltpu.VMEM((heads, dest, LANES), F32),
            pltpu.VMEM((heads, dest, LANES), F32),
            pltpu.VMEM((slots, heads, blk, blk), F32),
            pltpu.VMEM((slots, heads, blk, blk), F32),
            pltpu.VMEM((dest, width), F32),
            pltpu.VMEM((dest, LANES), F32),
            pltpu.VMEM((dest, LANES), BF16),
            pltpu.VMEM((sources, width), F32),
            pltpu.VMEM((blocks, heads, blk), F32),
            pltpu.VMEM((dest, LANES), F32),
        ],
        compiler_params=pltpu.CompilerParams(vmem_limit_bytes=52 * 1024 * 1024),
    )(rows, cols, counts, x_all, x_dst, weight, att_src, att_dst, grad_out, masks)


def unpack_weight(part, inputs):
    pieces = part.shape[0] // inputs
    return jnp.concatenate([part[g * inputs : (g + 1) * inputs] for g in range(pieces)], axis=1)


def shards(
    x_src, x_dst, weight, att_src, att_dst, grad_out, block_rows, block_cols, block_masks, block_counts
):
    heads, head_dim = att_src.shape
    x_all = lax.all_gather(x_src, "panel", axis=0, tiled=True)
    grad_dst, part_src, part_weight, part_att = layer(
        x_all, x_dst, weight, att_src, att_dst, grad_out, block_rows, block_cols, block_masks, block_counts
    )
    share = lax.psum_scatter(part_src.astype(F32), "panel", scatter_dimension=0, tiled=True)
    att = part_att[:8].astype(F32) + part_att[8:].astype(F32)
    grad_src = lax.psum(share, "rep")
    grad_weight, att = lax.psum(
        (unpack_weight(part_weight, weight.shape[0]).astype(F32), att), ("panel", "rep")
    )
    att = att.reshape(2, heads, head_dim)
    return grad_src, grad_dst, grad_weight, att[0], att[1]


def solution(mesh):
    both = P(("panel", "rep"))
    return jax.shard_map(
        shards,
        mesh=mesh,
        in_specs=(P("panel", None), both, P(), P(), P(), both, both, both, both, both),
        out_specs=(P("panel", None), both, P(), P(), P()),
        check_vma=False,
    )
```

```python
import jax
import jax.numpy as jnp
from jax import lax
from jax.experimental import pallas as pl
from jax.experimental.pallas import tpu as pltpu
from jax.sharding import PartitionSpec as P

F32 = jnp.float32
BF16 = jnp.bfloat16
MESH = pl.DeviceIdType.MESH
LANES = 128
CHUNK = 16


def mm(a, b, ca=1, cb=0):
    return lax.dot_general(a, b, (((ca,), (cb,)), ((), ())), preferred_element_type=F32)


def split(values, parts):
    pieces = []
    for _ in range(parts):
        piece = values.astype(BF16)
        pieces.append(piece)
        values = values - piece.astype(F32)
    return pieces


def mm_split(a, b, parts, ca=1, cb=0):
    return sum(mm(piece, b, ca, cb) for piece in split(a, parts))


def edge_terms(pre):
    small = jnp.exp(-jnp.abs(pre))
    grown = 1.0 + small
    inverse = 1.0 / grown
    sigma = 0.2 * pre + 0.8 * (jnp.maximum(pre, 0.0) + jnp.log(grown))
    sigmoid = jnp.where(pre >= 0.0, inverse, small * inverse)
    return jnp.exp(sigma), 0.2 + 0.8 * sigmoid


def iota(shape, dim):
    return lax.broadcasted_iota(jnp.int32, shape, dim)


def layer_kernel(
    rows_ref, cols_ref, count_ref, x_all_ref, x_dst_ref, weight_ref, att_src_ref, att_dst_ref,
    grad_ref, masks_ref,
    grad_dst_ref, part_ref, part_att_ref,
    proj_src, proj_dst, score_src, score_wide, inv_wide, weights, slopes,
    numer, denom, centre, grad_source, grad_score_src, grad_score_dst,
):
    heads, head_dim = att_src_ref.shape
    width = weight_ref.shape[1]
    pairs = width // LANES
    blk = masks_ref.shape[1]
    source_blocks = x_all_ref.shape[0] // blk
    dest = x_dst_ref.shape[0]
    count = count_ref[0]
    owners, share = part_ref.shape[1], part_ref.shape[2] - CHUNK
    reps = x_all_ref.shape[0] // source_blocks // share
    inputs = weight_ref.shape[0]

    lane_head = iota((heads, width), 1) // head_dim
    own = lane_head == iota((heads, width), 0)
    spread_src = jnp.where(own, jnp.concatenate([att_src_ref[...]] * heads, axis=1), 0.0)
    spread_dst = jnp.where(own, jnp.concatenate([att_dst_ref[...]] * heads, axis=1), 0.0)
    pad_rows = jnp.zeros((LANES - heads, width), F32)
    ones_heads = jnp.concatenate([jnp.where(own, 1.0, 0.0), pad_rows], axis=0).astype(BF16)
    tall_src = jnp.concatenate([spread_src, pad_rows], axis=0)
    tall_dst = jnp.concatenate([spread_dst, pad_rows], axis=0)

    for s in range(source_blocks):
        at = slice(s * blk, (s + 1) * blk)
        proj_src[at, :] = mm(x_all_ref[at, :], weight_ref[...]).astype(BF16)
    proj_dst[...] = mm(x_dst_ref[...], weight_ref[...]).astype(BF16)
    for s in range(source_blocks):
        at = slice(s * blk, (s + 1) * blk)
        stacked = jnp.concatenate([p.astype(F32) for p in split(spread_src, 3)], axis=0)
        got = mm(stacked.astype(BF16), proj_src[at, :], 1, 1)
        score_src[s] = got[:heads] + got[heads : 2 * heads] + got[2 * heads :]
    score_d = sum(mm(proj_dst[...], p, 1, 1) for p in split(tall_dst, 3))
    pre_self = score_d + sum(mm(proj_dst[...], p, 1, 1) for p in split(tall_src, 3))
    for h in range(heads):
        score_wide[h] = jnp.broadcast_to(score_d[:, h : h + 1], (dest, LANES))

    numer[...] = jnp.zeros_like(numer)
    denom[...] = jnp.zeros_like(denom)
    grad_source[...] = jnp.zeros_like(grad_source)
    grad_score_src[...] = jnp.zeros_like(grad_score_src)
    grad_score_dst[...] = jnp.zeros_like(grad_score_dst)

    low = (iota((1, LANES), 1) < head_dim).astype(F32).astype(BF16)
    high = (iota((1, LANES), 1) >= head_dim).astype(F32).astype(BF16)
    second = iota((2 * blk, LANES), 0) // blk
    lane = iota((2 * blk, LANES), 1)

    def both(values):
        return jnp.concatenate([values * low, values * high], axis=0)

    def pick(g, with_low):
        head = 2 * g + second
        hit = lane == head
        if with_low:
            hit = hit | (lane == head + heads)
        return jnp.where(hit, 1.0, 0.0)

    def forward(b, carry):
        r = pl.ds(pl.multiple_of(rows_ref[b] * blk, blk), blk)
        c = cols_ref[b]
        src = pl.ds(pl.multiple_of(c * blk, blk), blk)
        live = masks_ref[b] > 0
        scores = score_src[c]
        for g in range(pairs):
            at = slice(g * LANES, (g + 1) * LANES)
            found = []
            for h in (2 * g, 2 * g + 1):
                edge, slope = edge_terms(score_wide[h, r, :] + scores[h : h + 1, :])
                edge = jnp.where(live, edge, 0.0)
                weights[b, h] = edge
                slopes[b, h] = slope
                found.append(edge.astype(BF16))
            right = jnp.concatenate(
                [both(proj_src[src, at]), pick(g, False).astype(BF16)], axis=1
            )
            got = mm(jnp.concatenate(found, axis=1), right)
            numer[r, at] += got[:, :LANES]
            denom[r, :] += got[:, LANES:]
        return carry

    lax.fori_loop(0, count, forward, 0)

    feats = proj_dst[...].astype(F32)
    cotan = grad_ref[...].astype(F32)
    self_weight, self_slope = edge_terms(pre_self)
    inverse = 1.0 / (denom[...] + self_weight)
    total = numer[...] + mm_split(self_weight, ones_heads, 2) * feats
    narrow = mm_split(cotan * total, ones_heads, 2, 1, 1) * inverse
    lanes = iota((dest, LANES), 1)
    narrow = jnp.where(lanes < heads, narrow, 0.0)
    top = narrow.astype(BF16).astype(F32)
    centre[...] = (top + pltpu.roll(narrow - top, heads, 1)).astype(BF16)
    self_att = jnp.where(lanes < heads, self_weight * inverse, 0.0)
    self_pair = mm_split(cotan * feats, ones_heads, 2, 1, 1)
    self_grad = self_att * (self_pair - narrow) * self_slope
    for h in range(heads):
        inv_wide[h] = jnp.broadcast_to(inverse[:, h : h + 1], (dest, LANES))

    def backward(b, carry):
        r = pl.ds(pl.multiple_of(rows_ref[b] * blk, blk), blk)
        c = cols_ref[b]
        src = pl.ds(pl.multiple_of(c * blk, blk), blk)
        for g in range(pairs):
            at = slice(g * LANES, (g + 1) * LANES)
            cot = grad_ref[r, at]
            left = jnp.concatenate([cot, centre[r, :]], axis=1)
            right = jnp.concatenate(
                [both(proj_src[src, at]), (-pick(g, True)).astype(BF16)], axis=1
            )
            apart = mm(left, right, 1, 1)
            shares, grads, sums = [], [], []
            for q in range(2):
                h = 2 * g + q
                share = weights[b, h] * inv_wide[h, r, :]
                grad = share * apart[:, q * blk : (q + 1) * blk] * slopes[b, h]
                sums.append(jnp.sum(grad, axis=0, keepdims=True))
                shares.append(share.astype(BF16))
                grads.append(grad.astype(BF16))
            grad_score_src[c, 2 * g : 2 * g + 2, :] += jnp.concatenate(sums, axis=0)
            grad_score_dst[r, :] += mm(
                jnp.concatenate(grads, axis=1), pick(g, False).astype(BF16)
            )
            grad_source[src, at] += mm(jnp.concatenate(shares, axis=0), both(cot), 0, 0)
        return carry

    lax.fori_loop(0, count, backward, 0)

    score_grad = grad_score_dst[...] + self_grad
    self_grad_b = self_grad.astype(BF16)
    score_grad_b = score_grad.astype(BF16)
    flat = (
        mm_split(self_att, ones_heads, 2) * cotan
        + mm(self_grad_b, tall_src.astype(BF16))
        + mm(score_grad_b, tall_dst.astype(BF16))
    ).astype(BF16)
    grad_dst_ref[...] = mm(flat, weight_ref[...], 1, 1)
    part_weight = mm(x_dst_ref[...], flat, 0, 0)
    att_src_part = mm(self_grad_b, proj_dst[...], 0, 0)[:heads]
    att_dst_part = mm(score_grad_b, proj_dst[...], 0, 0)[:heads]

    spread_b = spread_src.astype(BF16)
    for s in range(source_blocks):
        at = slice(s * blk, (s + 1) * blk)
        scores = grad_score_src[s].astype(BF16)
        source = (grad_source[at, :] + mm(scores, spread_b, 0, 0)).astype(BF16)
        product = mm(source, weight_ref[...], 1, 1).astype(part_ref.dtype)
        for rep in range(reps):
            part_ref[s % 2, s // 2 * reps + rep, :share, :] = product[
                rep * share : (rep + 1) * share
            ]
        part_weight += mm(x_all_ref[at, :], source, 0, 0)
        att_src_part += mm(scores, proj_src[at, :])
    tiles = [
        part_weight[n : n + CHUNK, g * LANES : (g + 1) * LANES].astype(part_ref.dtype)
        for g in range(pairs)
        for n in range(0, inputs, CHUNK)
    ]
    half = len(tiles) // 2
    for core in range(2):
        for owner in range(owners):
            part_ref[core, owner, share:, :] = (
                tiles[core * half + owner] if owner < half else jnp.zeros((CHUNK, LANES), part_ref.dtype)
            )
    src_row = jnp.sum(jnp.where(own, att_src_part, 0.0), axis=0, keepdims=True)
    dst_row = jnp.sum(jnp.where(own, att_dst_part, 0.0), axis=0, keepdims=True)
    stack = [row[:, g * LANES : (g + 1) * LANES] for row in (src_row, dst_row) for g in range(pairs)]
    att = jnp.concatenate(stack, axis=0)
    part_att_ref[...] = jnp.concatenate(
        [att.astype(BF16).astype(F32), att - att.astype(BF16).astype(F32)], axis=0
    ).astype(part_att_ref.dtype)


def place():
    panel, rep = lax.axis_index("panel"), lax.axis_index("rep")
    return panel // 2, panel % 2, rep, lax.axis_size("panel") // 2, lax.axis_size("rep")


def remote(src, dst, send, recv, panel, rep):
    return pltpu.make_async_remote_copy(
        src_ref=src, dst_ref=dst, send_sem=send, recv_sem=recv, device_id=(panel, rep), device_id_type=MESH
    )


def each(start, stop, step):
    def body(k, carry):
        step(k)
        return carry

    lax.fori_loop(start, stop, body, 0)


def gather_kernel(x_ref, out_ref, send, recv, pass_send, pass_recv):
    plane, core, rep, planes, _ = place()
    me = plane * 2 + core
    mate = plane * 2 + 1 - core
    barrier = pltpu.get_barrier_semaphore()

    def peer(k):
        return lax.rem(plane + k, planes) * 2 + core

    def greet(k):
        pl.semaphore_signal(barrier, inc=1, device_id=(peer(k), rep), device_id_type=MESH)

    each(1, planes, greet)
    pl.semaphore_signal(barrier, inc=1, device_id=(mate, rep), device_id_type=MESH)
    pl.semaphore_wait(barrier, planes)

    def own(k):
        return remote(x_ref, out_ref.at[me], send.at[k], recv.at[k], peer(k), rep)

    def passed(k):
        slot = lax.rem(plane + planes - k, planes) * 2 + core
        return remote(out_ref.at[slot], out_ref.at[slot], pass_send.at[k], pass_recv.at[k], mate, rep)

    each(1, planes, lambda k: own(k).start())
    first = remote(x_ref, out_ref.at[me], pass_send.at[0], pass_recv.at[0], mate, rep)
    first.start()
    out_ref[me] = x_ref[...]

    def hand_on(k):
        own(k).wait_recv()
        passed(k).start()

    each(1, planes, hand_on)
    first.wait()

    def finish(k):
        own(k).wait_send()
        passed(k).wait()

    each(1, planes, finish)


def gather(x_src):
    panels = lax.axis_size("panel")
    sems = pltpu.SemaphoreType.DMA((panels // 2,))
    vmem = pl.BlockSpec(memory_space=pltpu.VMEM)
    out = pl.pallas_call(
        gather_kernel,
        out_shape=jax.ShapeDtypeStruct((panels,) + x_src.shape, x_src.dtype),
        in_specs=[vmem],
        out_specs=vmem,
        scratch_shapes=[sems] * 4,
        compiler_params=pltpu.CompilerParams(collective_id=0, has_side_effects=True),
    )(x_src)
    return out.reshape(panels * x_src.shape[0], x_src.shape[1])


def reduce_kernel(
    part_ref, att_ref, grad_src_ref, grad_weight_ref, att_src_ref, att_dst_ref,
    mate_part, mate_att, merged, landed, chunks, chunk, mate_sems, send, recv, row_send, row_recv,
    chunk_send, chunk_recv,
):
    plane, core, rep, planes, reps = place()
    owners, rows = merged.shape[:2]
    share = rows - 2 * CHUNK
    devices = 2 * owners
    me = plane * reps + rep
    panel = plane * 2 + core
    mate = plane * 2 + 1 - core
    index = panel * reps + rep
    barrier = pltpu.get_barrier_semaphore()

    def other(k):
        e = lax.rem(index + k, devices)
        return e // reps, lax.rem(e, reps)

    def greet(k):
        pl.semaphore_signal(barrier, inc=1, device_id=other(k), device_id_type=MESH)

    each(1, devices, greet)
    pl.semaphore_wait(barrier, devices - 1)

    swap = remote(part_ref.at[1 - core], mate_part, mate_sems.at[0], mate_sems.at[1], mate, rep)
    swap_att = remote(att_ref, mate_att, mate_sems.at[2], mate_sems.at[3], mate, rep)
    swap.start()
    swap_att.start()
    swap_att.wait()
    pair_att = att_ref[...].astype(F32) + mate_att[...].astype(F32)
    pair_att = pair_att[: CHUNK // 2] + pair_att[CHUNK // 2 :]
    top = pair_att.astype(BF16).astype(F32)
    tail = jnp.concatenate([top, pair_att - top], axis=0).astype(BF16)
    swap.wait()

    def to_owner(k):
        d = lax.rem(me + k, owners)
        return remote(
            merged.at[d], landed.at[k], send.at[k], recv.at[k], d // reps * 2 + core, lax.rem(d, reps)
        )

    def merge(k):
        d = lax.rem(me + k, owners)
        summed = part_ref[core, d].astype(F32) + mate_part[d].astype(F32)
        merged[d, : share + CHUNK, :] = summed.astype(BF16)
        merged[d, share + CHUNK :, :] = tail

    def merge_send(k):
        merge(k)
        to_owner(k).start()

    each(1, owners, merge_send)
    merge(0)

    def collect(k, total):
        to_owner(k).wait_recv()
        return total + landed[k].astype(F32)

    total = lax.fori_loop(1, owners, collect, merged[me].astype(F32))

    chunk[...] = total[share : share + CHUNK].astype(BF16)

    def spread(k):
        e_panel, e_rep = other(k)
        return remote(chunk, chunks.at[index], chunk_send.at[k], chunk_recv.at[k], e_panel, e_rep)

    def rows_to(k):
        part = grad_src_ref.at[pl.ds(pl.multiple_of(rep * share, share), share)]
        return remote(part, part, row_send.at[k], row_recv.at[k], panel, lax.rem(rep + k, reps))

    grad_src_ref[pl.ds(pl.multiple_of(rep * share, share), share), :] = total[:share]
    each(1, devices, lambda k: spread(k).start())
    each(1, reps, lambda k: rows_to(k).start())
    chunks[index] = chunk[...]
    att = total[share + CHUNK :]
    att = att[: CHUNK // 2] + att[CHUNK // 2 :]
    heads, head_dim = att_src_ref.shape
    per = LANES // head_dim
    lines = [
        att[r : r + 1, q * head_dim : (q + 1) * head_dim] for r in range(2 * heads // per) for q in range(per)
    ]
    att_src_ref[...] = jnp.concatenate(lines[:heads], axis=0)
    att_dst_ref[...] = jnp.concatenate(lines[heads:], axis=0)
    each(1, owners, lambda k: to_owner(k).wait_send())
    each(1, devices, lambda k: spread(k).wait())
    each(1, reps, lambda k: rows_to(k).wait())
    inputs, width = grad_weight_ref.shape
    half = inputs * width // LANES // CHUNK // 2
    for n in range(2 * half):
        c, d = n // half, n % half
        sender = (d // reps * 2 + c) * reps + d % reps
        at, col = n * CHUNK % inputs, n * CHUNK // inputs * LANES
        grad_weight_ref[at : at + CHUNK, col : col + LANES] = chunks[sender].astype(F32)


def reduce(part, part_att, inputs, width, heads, rows):
    owners, lines = part.shape[1:3]
    reps = lax.axis_size("rep")
    vmem = pl.BlockSpec(memory_space=pltpu.VMEM)
    dma = pltpu.SemaphoreType.DMA
    return pl.pallas_call(
        reduce_kernel,
        out_shape=(
            jax.ShapeDtypeStruct((rows, inputs), F32),
            jax.ShapeDtypeStruct((inputs, width), F32),
            jax.ShapeDtypeStruct((heads, width // heads), F32),
            jax.ShapeDtypeStruct((heads, width // heads), F32),
        ),
        in_specs=[vmem] * 2,
        out_specs=(vmem,) * 4,
        scratch_shapes=[
            pltpu.VMEM((owners, lines, LANES), BF16),
            pltpu.VMEM((CHUNK, LANES), BF16),
            pltpu.VMEM((owners, lines + CHUNK, LANES), BF16),
            pltpu.VMEM((owners, lines + CHUNK, LANES), BF16),
            pltpu.VMEM((2 * owners, CHUNK, LANES), BF16),
            pltpu.VMEM((CHUNK, LANES), BF16),
            dma((4,)),
            dma((owners,)),
            dma((owners,)),
            dma((reps,)),
            dma((reps,)),
            dma((2 * owners,)),
            dma((2 * owners,)),
        ],
        compiler_params=pltpu.CompilerParams(
            collective_id=1, has_side_effects=True, vmem_limit_bytes=32 * 1024 * 1024
        ),
    )(part, part_att)


def layer(x_all, x_dst, weight, att_src, att_dst, grad_out, rows, cols, masks, counts):
    heads = att_src.shape[0]
    inputs, width = weight.shape
    slots, blk = masks.shape[:2]
    sources, dest = x_all.shape[0], x_dst.shape[0]
    blocks = sources // blk
    reps = lax.axis_size("rep")
    owners = blocks // 2 * reps
    vmem = pl.BlockSpec(memory_space=pltpu.VMEM)
    smem = pl.BlockSpec(memory_space=pltpu.SMEM)
    return pl.pallas_call(
        layer_kernel,
        out_shape=(
            jax.ShapeDtypeStruct((dest, inputs), F32),
            jax.ShapeDtypeStruct((2, owners, blk // reps + CHUNK, LANES), BF16),
            jax.ShapeDtypeStruct((CHUNK, LANES), BF16),
        ),
        in_specs=[smem] * 3 + [vmem] * 7,
        out_specs=(vmem,) * 3,
        scratch_shapes=[
            pltpu.VMEM((sources, width), BF16),
            pltpu.VMEM((dest, width), BF16),
            pltpu.VMEM((blocks, heads, blk), F32),
            pltpu.VMEM((heads, dest, LANES), F32),
            pltpu.VMEM((heads, dest, LANES), F32),
            pltpu.VMEM((slots, heads, blk, blk), F32),
            pltpu.VMEM((slots, heads, blk, blk), F32),
            pltpu.VMEM((dest, width), F32),
            pltpu.VMEM((dest, LANES), F32),
            pltpu.VMEM((dest, LANES), BF16),
            pltpu.VMEM((sources, width), F32),
            pltpu.VMEM((blocks, heads, blk), F32),
            pltpu.VMEM((dest, LANES), F32),
        ],
        compiler_params=pltpu.CompilerParams(vmem_limit_bytes=52 * 1024 * 1024),
    )(rows, cols, counts, x_all, x_dst, weight, att_src, att_dst, grad_out, masks)


def shards(
    x_src, x_dst, weight, att_src, att_dst, grad_out, block_rows, block_cols, block_masks, block_counts
):
    x_all = gather(x_src)
    grad_dst, part, part_att = layer(
        x_all, x_dst, weight, att_src, att_dst, grad_out, block_rows, block_cols, block_masks, block_counts
    )
    grad_src, grad_weight, grad_att_src, grad_att_dst = reduce(
        part, part_att, weight.shape[0], weight.shape[1], att_src.shape[0], x_src.shape[0]
    )
    return grad_src, grad_dst, grad_weight, grad_att_src, grad_att_dst


def solution(mesh):
    both = P(("panel", "rep"))
    return jax.shard_map(
        shards,
        mesh=mesh,
        in_specs=(P("panel", None), both, P(), P(), P(), both, both, both, both, both),
        out_specs=(P("panel", None), both, P(), P(), P()),
        check_vma=False,
    )
```

```python
import jax
import jax.numpy as jnp
from jax import lax
from jax.experimental import pallas as pl
from jax.experimental.pallas import tpu as pltpu
from jax.sharding import PartitionSpec as P

F32 = jnp.float32
BF16 = jnp.bfloat16
MESH = pl.DeviceIdType.MESH
LANES = 128
CHUNK = 16
LOG2_E = 1.4426950408889634


def mm(a, b, ca=1, cb=0):
    return lax.dot_general(a, b, (((ca,), (cb,)), ((), ())), preferred_element_type=F32)


def split(values, parts):
    pieces = []
    for _ in range(parts):
        piece = values.astype(BF16)
        pieces.append(piece)
        values = values - piece.astype(F32)
    return pieces


def mm_split(a, b, parts, ca=1, cb=0):
    return sum(mm(piece, b, ca, cb) for piece in split(a, parts))


def edge_terms(pre):
    grown = 1.0 + jnp.exp2(-jnp.abs(pre))
    sigma = jnp.maximum(pre, 0.2 * pre) + 0.8 * jnp.log2(grown)
    return jnp.exp2(sigma), 0.6 + 0.4 * jnp.tanh((0.5 / LOG2_E) * pre)


def iota(shape, dim):
    return lax.broadcasted_iota(jnp.int32, shape, dim)


def layer_kernel(
    rows_ref, cols_ref, count_ref, x_all_ref, x_dst_ref, weight_ref, att_src_ref, att_dst_ref,
    grad_ref, masks_ref,
    grad_dst_ref, part_ref, part_att_ref,
    proj_src, proj_turned, proj_dst, cotan_turned, score_src, score_wide, inv_wide, weights, slopes,
    numer, denom, centre, grad_source, grad_score_src, grad_score_dst,
):
    heads, head_dim = att_src_ref.shape
    width = weight_ref.shape[1]
    pairs = width // LANES
    blk = masks_ref.shape[1]
    source_blocks = x_all_ref.shape[0] // blk
    dest = x_dst_ref.shape[0]
    count = count_ref[0]
    owners, share = part_ref.shape[1], part_ref.shape[2] - CHUNK
    reps = x_all_ref.shape[0] // source_blocks // share
    inputs = weight_ref.shape[0]

    lane_head = iota((heads, width), 1) // head_dim
    own = lane_head == iota((heads, width), 0)
    spread_src = jnp.where(own, jnp.concatenate([att_src_ref[...]] * heads, axis=1), 0.0)
    spread_dst = jnp.where(own, jnp.concatenate([att_dst_ref[...]] * heads, axis=1), 0.0)
    pad_rows = jnp.zeros((LANES - heads, width), F32)
    ones_heads = jnp.concatenate([jnp.where(own, 1.0, 0.0), pad_rows], axis=0).astype(BF16)
    ones_turned = jnp.where(
        iota((width, LANES), 0) // head_dim == iota((width, LANES), 1), 1.0, 0.0
    ).astype(BF16)
    tall_src = jnp.concatenate([spread_src, pad_rows], axis=0)
    tall_dst = jnp.concatenate([spread_dst, pad_rows], axis=0)

    stack_src = jnp.concatenate([p.astype(F32) for p in split(spread_src, 3)], axis=0)
    stack_dst = jnp.concatenate([p.astype(F32) for p in split(spread_dst, 3)], axis=0)
    stacked = stack_src.astype(BF16)
    weight_turned = weight_ref[...].T
    for s in range(source_blocks):
        at = slice(s * blk, (s + 1) * blk)
        proj_src[at, :] = mm(x_all_ref[at, :], weight_ref[...]).astype(BF16)
        turned = mm(weight_turned, x_all_ref[at, :], 1, 1).astype(BF16)
        proj_turned[s] = turned
        got = mm(stacked, turned)
        score_src[s] = (got[:heads] + got[heads : 2 * heads] + got[2 * heads :]) * LOG2_E
    proj_dst[...] = mm(x_dst_ref[...], weight_ref[...]).astype(BF16)
    stacked = jnp.concatenate(
        [stack_dst, stack_src, jnp.zeros((LANES - 6 * heads, width), F32)], axis=0
    ).astype(BF16)
    got = mm(proj_dst[...], stacked, 1, 1) * LOG2_E
    shift = [got] + [pltpu.roll(got, LANES - n * heads, 1) for n in range(1, 6)]
    score_d = shift[0] + shift[1] + shift[2]
    pre_self = score_d + (shift[3] + shift[4] + shift[5])
    for h in range(heads):
        score_wide[h] = jnp.broadcast_to(score_d[:, h : h + 1], (dest, LANES))
    for d in range(dest // blk):
        cotan_turned[d] = grad_ref[d * blk : (d + 1) * blk, :].T

    numer[...] = jnp.zeros_like(numer)
    denom[...] = jnp.zeros_like(denom)
    grad_source[...] = jnp.zeros_like(grad_source)
    grad_score_src[...] = jnp.zeros_like(grad_score_src)
    grad_score_dst[...] = jnp.zeros_like(grad_score_dst)

    low = (iota((1, LANES), 1) < head_dim).astype(F32).astype(BF16)
    high = (iota((1, LANES), 1) >= head_dim).astype(F32).astype(BF16)
    second = iota((2 * blk, LANES), 0) // blk
    lane = iota((2 * blk, LANES), 1)

    def both(values):
        return jnp.concatenate([values * low, values * high], axis=0)

    ones_pair = [jnp.where(lane == 2 * g + second, 1.0, 0.0).astype(BF16) for g in range(pairs)]
    column = iota((LANES, 2 * blk), 0)
    column_head = iota((LANES, 2 * blk), 1) // blk
    minus_pair = [
        jnp.where(lax.rem(column, heads) == 2 * g + column_head, -1.0, 0.0) for g in range(pairs)
    ]
    minus_pair = [jnp.where(column < 2 * heads, m, 0.0).astype(BF16) for m in minus_pair]

    def forward(b, carry):
        r = pl.ds(pl.multiple_of(rows_ref[b] * blk, blk), blk)
        c = cols_ref[b]
        src = pl.ds(pl.multiple_of(c * blk, blk), blk)
        live = masks_ref[b] > 0
        scores = score_src[c]
        for g in range(pairs):
            at = slice(g * LANES, (g + 1) * LANES)
            found = []
            for h in (2 * g, 2 * g + 1):
                edge, slope = edge_terms(score_wide[h, r, :] + scores[h : h + 1, :])
                edge = jnp.where(live, edge, 0.0)
                weights[b, h] = edge
                slopes[b, h] = slope
                found.append(edge.astype(BF16))
            right = jnp.concatenate(
                [both(proj_src[src, at]), ones_pair[g]], axis=1
            )
            got = mm(jnp.concatenate(found, axis=1), right)
            numer[r, at] += got[:, :LANES]
            denom[r, :] += got[:, LANES:]
        return carry

    lax.fori_loop(0, count, forward, 0)

    feats = proj_dst[...].astype(F32)
    cotan = grad_ref[...].astype(F32)
    self_weight, self_slope = edge_terms(pre_self)
    inverse = 1.0 / (denom[...] + self_weight)
    total = numer[...] + mm_split(self_weight, ones_heads, 2) * feats
    narrow = mm_split(cotan * total, ones_turned, 2) * inverse
    lanes = iota((dest, LANES), 1)
    narrow = jnp.where(lanes < heads, narrow, 0.0)
    top = narrow.astype(BF16).astype(F32)
    centre[...] = (top + pltpu.roll(narrow - top, heads, 1)).astype(BF16)
    self_att = jnp.where(lanes < heads, self_weight * inverse, 0.0)
    self_pair = mm_split(cotan * feats, ones_turned, 2)
    self_grad = self_att * (self_pair - narrow) * self_slope
    for h in range(heads):
        inv_wide[h] = jnp.broadcast_to(inverse[:, h : h + 1], (dest, LANES))

    def backward(b, carry):
        d = rows_ref[b]
        r = pl.ds(pl.multiple_of(d * blk, blk), blk)
        c = cols_ref[b]
        nothing = jnp.zeros((head_dim, blk), BF16)
        for g in range(pairs):
            at = slice(g * LANES, (g + 1) * LANES)
            left = jnp.concatenate([grad_ref[r, at], centre[r, :]], axis=1)
            feats_turned = proj_turned[c, at, :]
            right = jnp.concatenate(
                [
                    jnp.concatenate([feats_turned[:head_dim], nothing], axis=1),
                    jnp.concatenate([nothing, feats_turned[head_dim:]], axis=1),
                    minus_pair[g],
                ],
                axis=0,
            )
            apart = mm(left, right)
            shares, sums = [], []
            for q in range(2):
                h = 2 * g + q
                share = weights[b, h] * inv_wide[h, r, :]
                grad = share * apart[:, q * blk : (q + 1) * blk] * slopes[b, h]
                sums.append(jnp.sum(grad, axis=0, keepdims=True))
                grad_score_dst[h, r, :] += grad
                shares.append(share.astype(BF16))
            grad_score_src[c, 2 * g : 2 * g + 2, :] += jnp.concatenate(sums, axis=0)
            got = mm(cotan_turned[d, at, :], jnp.concatenate(shares, axis=1))
            grad_source[c, at, :] += jnp.concatenate(
                [got[:head_dim, :blk], got[head_dim:, blk:]], axis=0
            )
        return carry

    lax.fori_loop(0, count, backward, 0)

    score_grad = self_grad
    for h in range(heads):
        score_grad += jnp.where(lanes == h, jnp.sum(grad_score_dst[h], axis=1, keepdims=True), 0.0)
    self_grad_b = self_grad.astype(BF16)
    score_grad_b = score_grad.astype(BF16)
    flat = (
        mm_split(self_att, ones_heads, 2) * cotan
        + mm(self_grad_b, tall_src.astype(BF16))
        + mm(score_grad_b, tall_dst.astype(BF16))
    ).astype(BF16)
    grad_dst_ref[...] = mm(flat, weight_ref[...], 1, 1)
    part_weight = mm(x_dst_ref[...], flat, 0, 0)
    att_src_part = mm(self_grad_b, proj_dst[...], 0, 0)[:heads]
    att_dst_part = mm(score_grad_b, proj_dst[...], 0, 0)[:heads]

    spread_turned = spread_src.T.astype(BF16)
    weight_turned_part = jnp.zeros((width, inputs), F32)
    for s in range(source_blocks):
        at = slice(s * blk, (s + 1) * blk)
        scores = grad_score_src[s].astype(BF16)
        source = (grad_source[s] + mm(spread_turned, scores)).astype(BF16)
        product = mm(weight_ref[...], source).T.astype(part_ref.dtype)
        for rep in range(reps):
            part_ref[s % 2, s // 2 * reps + rep, :share, :] = product[
                rep * share : (rep + 1) * share
            ]
        weight_turned_part += mm(source, x_all_ref[at, :])
        att_src_part += mm(scores, proj_src[at, :])
    part_weight += weight_turned_part.T
    tiles = [
        part_weight[n : n + CHUNK, g * LANES : (g + 1) * LANES].astype(part_ref.dtype)
        for g in range(pairs)
        for n in range(0, inputs, CHUNK)
    ]
    half = len(tiles) // 2
    for core in range(2):
        for owner in range(owners):
            part_ref[core, owner, share:, :] = (
                tiles[core * half + owner] if owner < half else jnp.zeros((CHUNK, LANES), part_ref.dtype)
            )
    src_row = jnp.sum(jnp.where(own, att_src_part, 0.0), axis=0, keepdims=True)
    dst_row = jnp.sum(jnp.where(own, att_dst_part, 0.0), axis=0, keepdims=True)
    stack = [row[:, g * LANES : (g + 1) * LANES] for row in (src_row, dst_row) for g in range(pairs)]
    att = jnp.concatenate(stack, axis=0)
    part_att_ref[...] = jnp.concatenate(
        [att.astype(BF16).astype(F32), att - att.astype(BF16).astype(F32)], axis=0
    ).astype(part_att_ref.dtype)


def place():
    panel, rep = lax.axis_index("panel"), lax.axis_index("rep")
    return panel // 2, panel % 2, rep, lax.axis_size("panel") // 2, lax.axis_size("rep")


def remote(src, dst, send, recv, panel, rep):
    return pltpu.make_async_remote_copy(
        src_ref=src, dst_ref=dst, send_sem=send, recv_sem=recv, device_id=(panel, rep), device_id_type=MESH
    )


def each(start, stop, step):
    def body(k, carry):
        step(k)
        return carry

    lax.fori_loop(start, stop, body, 0)


def gather_kernel(x_ref, out_ref, send, recv, pass_send, pass_recv):
    plane, core, rep, planes, _ = place()
    me = plane * 2 + core
    mate = plane * 2 + 1 - core
    barrier = pltpu.get_barrier_semaphore()

    def peer(k):
        return lax.rem(plane + k, planes) * 2 + core

    def greet(k):
        pl.semaphore_signal(barrier, inc=1, device_id=(peer(k), rep), device_id_type=MESH)

    each(1, planes, greet)
    pl.semaphore_signal(barrier, inc=1, device_id=(mate, rep), device_id_type=MESH)
    pl.semaphore_wait(barrier, planes)

    def own(k):
        return remote(x_ref, out_ref.at[me], send.at[k], recv.at[k], peer(k), rep)

    def passed(k):
        slot = lax.rem(plane + planes - k, planes) * 2 + core
        return remote(out_ref.at[slot], out_ref.at[slot], pass_send.at[k], pass_recv.at[k], mate, rep)

    each(1, planes, lambda k: own(k).start())
    first = remote(x_ref, out_ref.at[me], pass_send.at[0], pass_recv.at[0], mate, rep)
    first.start()
    out_ref[me] = x_ref[...]

    def hand_on(k):
        own(k).wait_recv()
        passed(k).start()

    each(1, planes, hand_on)
    first.wait()

    def finish(k):
        own(k).wait_send()
        passed(k).wait()

    each(1, planes, finish)


def gather(x_src):
    panels = lax.axis_size("panel")
    sems = pltpu.SemaphoreType.DMA((panels // 2,))
    vmem = pl.BlockSpec(memory_space=pltpu.VMEM)
    out = pl.pallas_call(
        gather_kernel,
        out_shape=jax.ShapeDtypeStruct((panels,) + x_src.shape, x_src.dtype),
        in_specs=[vmem],
        out_specs=vmem,
        scratch_shapes=[sems] * 4,
        compiler_params=pltpu.CompilerParams(collective_id=0, has_side_effects=True),
    )(x_src)
    return out.reshape(panels * x_src.shape[0], x_src.shape[1])


def reduce_kernel(
    part_ref, att_ref, grad_src_ref, grad_weight_ref, att_src_ref, att_dst_ref,
    mate_part, mate_att, merged, landed, chunks, chunk, mate_sems, send, recv, row_send, row_recv,
    chunk_send, chunk_recv,
):
    plane, core, rep, planes, reps = place()
    owners, rows = merged.shape[:2]
    share = rows - 2 * CHUNK
    devices = 2 * owners
    me = plane * reps + rep
    panel = plane * 2 + core
    mate = plane * 2 + 1 - core
    index = panel * reps + rep
    barrier = pltpu.get_barrier_semaphore()

    def other(k):
        e = lax.rem(index + k, devices)
        return e // reps, lax.rem(e, reps)

    def greet(k):
        pl.semaphore_signal(barrier, inc=1, device_id=other(k), device_id_type=MESH)

    each(1, devices, greet)
    pl.semaphore_wait(barrier, devices - 1)

    swap = remote(part_ref.at[1 - core], mate_part, mate_sems.at[0], mate_sems.at[1], mate, rep)
    swap_att = remote(att_ref, mate_att, mate_sems.at[2], mate_sems.at[3], mate, rep)
    swap.start()
    swap_att.start()
    swap_att.wait()
    pair_att = att_ref[...].astype(F32) + mate_att[...].astype(F32)
    pair_att = pair_att[: CHUNK // 2] + pair_att[CHUNK // 2 :]
    top = pair_att.astype(BF16).astype(F32)
    tail = jnp.concatenate([top, pair_att - top], axis=0).astype(BF16)
    swap.wait()

    def to_owner(k):
        d = lax.rem(me + k, owners)
        return remote(
            merged.at[d], landed.at[k], send.at[k], recv.at[k], d // reps * 2 + core, lax.rem(d, reps)
        )

    def merge(k):
        d = lax.rem(me + k, owners)
        summed = part_ref[core, d].astype(F32) + mate_part[d].astype(F32)
        merged[d, : share + CHUNK, :] = summed.astype(BF16)
        merged[d, share + CHUNK :, :] = tail

    def merge_send(k):
        merge(k)
        to_owner(k).start()

    each(1, owners, merge_send)
    merge(0)

    def collect(k, total):
        to_owner(k).wait_recv()
        return total + landed[k].astype(F32)

    total = lax.fori_loop(1, owners, collect, merged[me].astype(F32))

    chunk[...] = total[share : share + CHUNK].astype(BF16)

    def spread(k):
        e_panel, e_rep = other(k)
        return remote(chunk, chunks.at[index], chunk_send.at[k], chunk_recv.at[k], e_panel, e_rep)

    def rows_to(k):
        part = grad_src_ref.at[pl.ds(pl.multiple_of(rep * share, share), share)]
        return remote(part, part, row_send.at[k], row_recv.at[k], panel, lax.rem(rep + k, reps))

    grad_src_ref[pl.ds(pl.multiple_of(rep * share, share), share), :] = total[:share]
    each(1, devices, lambda k: spread(k).start())
    each(1, reps, lambda k: rows_to(k).start())
    chunks[index] = chunk[...]
    att = total[share + CHUNK :]
    att = att[: CHUNK // 2] + att[CHUNK // 2 :]
    heads, head_dim = att_src_ref.shape
    per = LANES // head_dim
    lines = [
        att[r : r + 1, q * head_dim : (q + 1) * head_dim] for r in range(2 * heads // per) for q in range(per)
    ]
    att_src_ref[...] = jnp.concatenate(lines[:heads], axis=0)
    att_dst_ref[...] = jnp.concatenate(lines[heads:], axis=0)
    each(1, owners, lambda k: to_owner(k).wait_send())
    each(1, devices, lambda k: spread(k).wait())
    each(1, reps, lambda k: rows_to(k).wait())
    inputs, width = grad_weight_ref.shape
    half = inputs * width // LANES // CHUNK // 2
    for n in range(2 * half):
        c, d = n // half, n % half
        sender = (d // reps * 2 + c) * reps + d % reps
        at, col = n * CHUNK % inputs, n * CHUNK // inputs * LANES
        grad_weight_ref[at : at + CHUNK, col : col + LANES] = chunks[sender].astype(F32)


def reduce(part, part_att, inputs, width, heads, rows):
    owners, lines = part.shape[1:3]
    reps = lax.axis_size("rep")
    vmem = pl.BlockSpec(memory_space=pltpu.VMEM)
    dma = pltpu.SemaphoreType.DMA
    return pl.pallas_call(
        reduce_kernel,
        out_shape=(
            jax.ShapeDtypeStruct((rows, inputs), F32),
            jax.ShapeDtypeStruct((inputs, width), F32),
            jax.ShapeDtypeStruct((heads, width // heads), F32),
            jax.ShapeDtypeStruct((heads, width // heads), F32),
        ),
        in_specs=[vmem] * 2,
        out_specs=(vmem,) * 4,
        scratch_shapes=[
            pltpu.VMEM((owners, lines, LANES), BF16),
            pltpu.VMEM((CHUNK, LANES), BF16),
            pltpu.VMEM((owners, lines + CHUNK, LANES), BF16),
            pltpu.VMEM((owners, lines + CHUNK, LANES), BF16),
            pltpu.VMEM((2 * owners, CHUNK, LANES), BF16),
            pltpu.VMEM((CHUNK, LANES), BF16),
            dma((4,)),
            dma((owners,)),
            dma((owners,)),
            dma((reps,)),
            dma((reps,)),
            dma((2 * owners,)),
            dma((2 * owners,)),
        ],
        compiler_params=pltpu.CompilerParams(
            collective_id=1, has_side_effects=True, vmem_limit_bytes=32 * 1024 * 1024
        ),
    )(part, part_att)


def layer(x_all, x_dst, weight, att_src, att_dst, grad_out, rows, cols, masks, counts):
    heads = att_src.shape[0]
    inputs, width = weight.shape
    slots, blk = masks.shape[:2]
    sources, dest = x_all.shape[0], x_dst.shape[0]
    blocks = sources // blk
    reps = lax.axis_size("rep")
    owners = blocks // 2 * reps
    vmem = pl.BlockSpec(memory_space=pltpu.VMEM)
    smem = pl.BlockSpec(memory_space=pltpu.SMEM)
    return pl.pallas_call(
        layer_kernel,
        out_shape=(
            jax.ShapeDtypeStruct((dest, inputs), F32),
            jax.ShapeDtypeStruct((2, owners, blk // reps + CHUNK, LANES), BF16),
            jax.ShapeDtypeStruct((CHUNK, LANES), BF16),
        ),
        in_specs=[smem] * 3 + [vmem] * 7,
        out_specs=(vmem,) * 3,
        scratch_shapes=[
            pltpu.VMEM((sources, width), BF16),
            pltpu.VMEM((blocks, width, blk), BF16),
            pltpu.VMEM((dest, width), BF16),
            pltpu.VMEM((dest // blk, width, blk), BF16),
            pltpu.VMEM((blocks, heads, blk), F32),
            pltpu.VMEM((heads, dest, LANES), F32),
            pltpu.VMEM((heads, dest, LANES), F32),
            pltpu.VMEM((slots, heads, blk, blk), F32),
            pltpu.VMEM((slots, heads, blk, blk), F32),
            pltpu.VMEM((dest, width), F32),
            pltpu.VMEM((dest, LANES), F32),
            pltpu.VMEM((dest, LANES), BF16),
            pltpu.VMEM((blocks, width, blk), F32),
            pltpu.VMEM((blocks, heads, blk), F32),
            pltpu.VMEM((heads, dest, LANES), F32),
        ],
        compiler_params=pltpu.CompilerParams(vmem_limit_bytes=62 * 1024 * 1024),
    )(rows, cols, counts, x_all, x_dst, weight, att_src, att_dst, grad_out, masks)


def shards(
    x_src, x_dst, weight, att_src, att_dst, grad_out, block_rows, block_cols, block_masks, block_counts
):
    x_all = gather(x_src)
    grad_dst, part, part_att = layer(
        x_all, x_dst, weight, att_src, att_dst, grad_out, block_rows, block_cols, block_masks, block_counts
    )
    grad_src, grad_weight, grad_att_src, grad_att_dst = reduce(
        part, part_att, weight.shape[0], weight.shape[1], att_src.shape[0], x_src.shape[0]
    )
    return grad_src, grad_dst, grad_weight, grad_att_src, grad_att_dst


def solution(mesh):
    both = P(("panel", "rep"))
    return jax.shard_map(
        shards,
        mesh=mesh,
        in_specs=(P("panel", None), both, P(), P(), P(), both, both, both, both, both),
        out_specs=(P("panel", None), both, P(), P(), P()),
        check_vma=False,
    )
```

```python
import jax
import jax.numpy as jnp
from jax import lax
from jax.experimental import pallas as pl
from jax.experimental.pallas import tpu as pltpu
from jax.sharding import PartitionSpec as P

F32 = jnp.float32
BF16 = jnp.bfloat16
MESH = pl.DeviceIdType.MESH
LANES = 128
CHUNK = 16
LOG2_E = 1.4426950408889634


def mm(a, b, ca=1, cb=0):
    return lax.dot_general(a, b, (((ca,), (cb,)), ((), ())), preferred_element_type=F32)


def split(values, parts):
    pieces = []
    for _ in range(parts):
        piece = values.astype(BF16)
        pieces.append(piece)
        values = values - piece.astype(F32)
    return pieces


def mm_split(a, b, parts, ca=1, cb=0):
    return sum(mm(piece, b, ca, cb) for piece in split(a, parts))


def edge_terms(pre):
    grown = 1.0 + jnp.exp2(-jnp.abs(pre))
    sigma = jnp.maximum(pre, 0.2 * pre) + 0.8 * jnp.log2(grown)
    return jnp.exp2(sigma), 0.6 + 0.4 * jnp.tanh((0.5 / LOG2_E) * pre)


def iota(shape, dim):
    return lax.broadcasted_iota(jnp.int32, shape, dim)


def layer_kernel(
    rows_ref, cols_ref, count_ref, x_all_ref, x_dst_ref, weight_ref, att_src_ref, att_dst_ref,
    grad_ref, masks_ref,
    grad_dst_ref, part_ref, part_att_ref,
    proj_src, proj_turned, proj_dst, cotan_turned, score_src, score_wide, inv_wide, weights, slopes,
    numer, denom, centre, grad_source, grad_score_src, grad_score_dst, source,
):
    heads, head_dim = att_src_ref.shape
    width = weight_ref.shape[1]
    pairs = width // LANES
    blk = masks_ref.shape[1]
    source_blocks = x_all_ref.shape[0] // blk
    dest = x_dst_ref.shape[0]
    count = count_ref[0]
    owners, share = part_ref.shape[1], part_ref.shape[2] - CHUNK
    reps = x_all_ref.shape[0] // source_blocks // share
    inputs = weight_ref.shape[0]

    lane_head = iota((heads, width), 1) // head_dim
    own = lane_head == iota((heads, width), 0)
    spread_src = jnp.where(own, jnp.concatenate([att_src_ref[...]] * heads, axis=1), 0.0)
    spread_dst = jnp.where(own, jnp.concatenate([att_dst_ref[...]] * heads, axis=1), 0.0)
    pad_rows = jnp.zeros((LANES - heads, width), F32)
    row = iota((LANES, width), 0)
    ones_heads = jnp.where(
        (lax.rem(row, heads) == iota((LANES, width), 1) // head_dim) & (row < 2 * heads), 1.0, 0.0
    ).astype(BF16)
    ones_turned = jnp.where(
        iota((width, LANES), 0) // head_dim == iota((width, LANES), 1), 1.0, 0.0
    ).astype(BF16)
    tall = jnp.concatenate([spread_src, spread_dst, pad_rows[heads:]], axis=0).astype(BF16)

    stack_src = jnp.concatenate([p.astype(F32) for p in split(spread_src, 3)], axis=0)
    stack_dst = jnp.concatenate([p.astype(F32) for p in split(spread_dst, 3)], axis=0)
    stacked = stack_src.astype(BF16)
    weight_turned = weight_ref[...].T
    proj_src[...] = mm(x_all_ref[...], weight_ref[...]).astype(BF16)
    per = min(4, source_blocks)
    for s in range(0, source_blocks, per):
        turned = mm(weight_turned, x_all_ref[s * blk : (s + per) * blk, :], 1, 1).astype(BF16)
        got = mm(stacked, turned)
        got = (got[:heads] + got[heads : 2 * heads] + got[2 * heads :]) * LOG2_E
        for n in range(per):
            proj_turned[s + n] = turned[:, n * blk : (n + 1) * blk]
            score_src[s + n] = got[:, n * blk : (n + 1) * blk]
    proj_dst[...] = mm(x_dst_ref[...], weight_ref[...]).astype(BF16)
    stacked = jnp.concatenate(
        [stack_dst, stack_src, jnp.zeros((LANES - 6 * heads, width), F32)], axis=0
    ).astype(BF16)
    got = mm(proj_dst[...], stacked, 1, 1) * LOG2_E
    shift = [got] + [pltpu.roll(got, LANES - n * heads, 1) for n in range(1, 6)]
    score_d = shift[0] + shift[1] + shift[2]
    pre_self = score_d + (shift[3] + shift[4] + shift[5])
    for h in range(heads):
        score_wide[h] = jnp.broadcast_to(score_d[:, h : h + 1], (dest, LANES))
    for d in range(dest // blk):
        cotan_turned[d] = grad_ref[d * blk : (d + 1) * blk, :].T

    numer[...] = jnp.zeros_like(numer)
    denom[...] = jnp.zeros_like(denom)
    grad_source[...] = jnp.zeros_like(grad_source)
    grad_score_src[...] = jnp.zeros_like(grad_score_src)
    grad_score_dst[...] = jnp.zeros_like(grad_score_dst)

    low = (iota((1, LANES), 1) < head_dim).astype(F32).astype(BF16)
    high = (iota((1, LANES), 1) >= head_dim).astype(F32).astype(BF16)
    second = iota((2 * blk, LANES), 0) // blk
    lane = iota((2 * blk, LANES), 1)

    def both(values):
        return jnp.concatenate([values * low, values * high], axis=0)

    ones_pair = [jnp.where(lane == 2 * g + second, 1.0, 0.0).astype(BF16) for g in range(pairs)]
    column = iota((LANES, 2 * blk), 0)
    column_head = iota((LANES, 2 * blk), 1) // blk
    minus_pair = [
        jnp.where(lax.rem(column, heads) == 2 * g + column_head, -1.0, 0.0) for g in range(pairs)
    ]
    minus_pair = [jnp.where(column < 2 * heads, m, 0.0).astype(BF16) for m in minus_pair]

    def forward(b, carry):
        r = pl.ds(pl.multiple_of(rows_ref[b] * blk, blk), blk)
        c = cols_ref[b]
        src = pl.ds(pl.multiple_of(c * blk, blk), blk)
        live = masks_ref[b] > 0
        scores = score_src[c]
        for g in range(pairs):
            at = slice(g * LANES, (g + 1) * LANES)
            found = []
            for h in (2 * g, 2 * g + 1):
                edge, slope = edge_terms(score_wide[h, r, :] + scores[h : h + 1, :])
                edge = jnp.where(live, edge, 0.0)
                weights[b, h] = edge
                slopes[b, h] = slope
                found.append(edge.astype(BF16))
            right = jnp.concatenate(
                [both(proj_src[src, at]), ones_pair[g]], axis=1
            )
            got = mm(jnp.concatenate(found, axis=1), right)
            numer[r, at] += got[:, :LANES]
            denom[r, :] += got[:, LANES:]
        return carry

    lax.fori_loop(0, count, forward, 0)

    lanes = iota((dest, LANES), 1)

    def two_pieces(values):
        top = values.astype(BF16).astype(F32)
        return (top + pltpu.roll(values - top, heads, 1)).astype(BF16)

    def over_heads(values):
        return jnp.where(lanes < heads, values, 0.0)

    feats = proj_dst[...].astype(F32)
    cotan = grad_ref[...].astype(F32)
    self_weight, self_slope = edge_terms(pre_self)
    self_weight = over_heads(self_weight)
    inverse = 1.0 / (denom[...] + jnp.where(lanes < heads, self_weight, 1.0))
    total = numer[...] + mm(two_pieces(self_weight), ones_heads) * feats
    attended = total * mm(two_pieces(over_heads(inverse)), ones_heads)
    narrow = over_heads(mm_split(cotan * attended, ones_turned, 2))
    centre[...] = two_pieces(narrow)
    self_att = self_weight * inverse
    self_pair = mm_split(cotan * feats, ones_turned, 2)
    self_grad = self_att * (self_pair - narrow) * self_slope
    for h in range(heads):
        inv_wide[h] = jnp.broadcast_to(inverse[:, h : h + 1], (dest, LANES))

    def backward(b, carry):
        d = rows_ref[b]
        r = pl.ds(pl.multiple_of(d * blk, blk), blk)
        c = cols_ref[b]
        nothing = jnp.zeros((head_dim, blk), BF16)
        for g in range(pairs):
            at = slice(g * LANES, (g + 1) * LANES)
            left = jnp.concatenate([grad_ref[r, at], centre[r, :]], axis=1)
            feats_turned = proj_turned[c, at, :]
            right = jnp.concatenate(
                [
                    jnp.concatenate([feats_turned[:head_dim], nothing], axis=1),
                    jnp.concatenate([nothing, feats_turned[head_dim:]], axis=1),
                    minus_pair[g],
                ],
                axis=0,
            )
            apart = mm(left, right)
            shares, sums = [], []
            for q in range(2):
                h = 2 * g + q
                share = weights[b, h] * inv_wide[h, r, :]
                grad = share * apart[:, q * blk : (q + 1) * blk] * slopes[b, h]
                sums.append(jnp.sum(grad, axis=0, keepdims=True))
                grad_score_dst[h, r, :] += grad
                shares.append(share.astype(BF16))
            grad_score_src[c, 2 * g : 2 * g + 2, :] += jnp.concatenate(sums, axis=0)
            got = mm(cotan_turned[d, at, :], jnp.concatenate(shares, axis=1))
            grad_source[c, at, :] += jnp.concatenate(
                [got[:head_dim, :blk], got[head_dim:, blk:]], axis=0
            )
        return carry

    lax.fori_loop(0, count, backward, 0)

    score_grad = self_grad
    for h in range(heads):
        score_grad += jnp.where(lanes == h, jnp.sum(grad_score_dst[h], axis=1, keepdims=True), 0.0)
    grads = (self_grad + pltpu.roll(score_grad, heads, 1)).astype(BF16)
    flat = (mm(two_pieces(self_att), ones_heads) * cotan + mm(grads, tall)).astype(BF16)
    grad_dst_ref[...] = mm(flat, weight_ref[...], 1, 1)
    part_weight = mm(x_dst_ref[...], flat, 0, 0)
    att_part = mm(grads, proj_dst[...], 0, 0)

    scores = jnp.concatenate([grad_score_src[s] for s in range(source_blocks)], axis=1).astype(BF16)
    spread_turned = spread_src.T.astype(BF16)
    for s in range(source_blocks):
        at = slice(s * blk, (s + 1) * blk)
        source[:, at] = (grad_source[s] + mm(spread_turned, scores[:, at])).astype(BF16)
    weight_turned_part = mm(source[...], x_all_ref[...])
    att_src_part = att_part[:heads] + mm(scores, proj_src[...])
    att_dst_part = att_part[heads : 2 * heads]
    for s in range(0, source_blocks, per):
        product = mm(weight_ref[...], source[:, s * blk : (s + per) * blk])
        for n in range(s, s + per):
            block = product[:, (n - s) * blk : (n - s + 1) * blk].T.astype(part_ref.dtype)
            for rep in range(reps):
                part_ref[n % 2, n // 2 * reps + rep, :share, :] = block[rep * share : (rep + 1) * share]
    part_weight += weight_turned_part.T
    tiles = [
        part_weight[n : n + CHUNK, g * LANES : (g + 1) * LANES].astype(part_ref.dtype)
        for g in range(pairs)
        for n in range(0, inputs, CHUNK)
    ]
    half = len(tiles) // 2
    for core in range(2):
        for owner in range(owners):
            part_ref[core, owner, share:, :] = (
                tiles[core * half + owner] if owner < half else jnp.zeros((CHUNK, LANES), part_ref.dtype)
            )
    src_row = jnp.sum(jnp.where(own, att_src_part, 0.0), axis=0, keepdims=True)
    dst_row = jnp.sum(jnp.where(own, att_dst_part, 0.0), axis=0, keepdims=True)
    stack = [row[:, g * LANES : (g + 1) * LANES] for row in (src_row, dst_row) for g in range(pairs)]
    att = jnp.concatenate(stack, axis=0)
    part_att_ref[...] = jnp.concatenate(
        [att.astype(BF16).astype(F32), att - att.astype(BF16).astype(F32)], axis=0
    ).astype(part_att_ref.dtype)


def place():
    panel, rep = lax.axis_index("panel"), lax.axis_index("rep")
    return panel // 2, panel % 2, rep, lax.axis_size("panel") // 2, lax.axis_size("rep")


def remote(src, dst, send, recv, panel, rep):
    return pltpu.make_async_remote_copy(
        src_ref=src, dst_ref=dst, send_sem=send, recv_sem=recv, device_id=(panel, rep), device_id_type=MESH
    )


def each(start, stop, step):
    def body(k, carry):
        step(k)
        return carry

    lax.fori_loop(start, stop, body, 0)


def gather_kernel(x_ref, out_ref, send, recv, pass_send, pass_recv):
    plane, core, rep, planes, _ = place()
    me = plane * 2 + core
    mate = plane * 2 + 1 - core
    barrier = pltpu.get_barrier_semaphore()

    def peer(k):
        return lax.rem(plane + k, planes) * 2 + core

    def greet(k):
        pl.semaphore_signal(barrier, inc=1, device_id=(peer(k), rep), device_id_type=MESH)

    each(1, planes, greet)
    pl.semaphore_signal(barrier, inc=1, device_id=(mate, rep), device_id_type=MESH)
    pl.semaphore_wait(barrier, planes)

    def own(k):
        return remote(x_ref, out_ref.at[me], send.at[k], recv.at[k], peer(k), rep)

    def passed(k):
        slot = lax.rem(plane + planes - k, planes) * 2 + core
        return remote(out_ref.at[slot], out_ref.at[slot], pass_send.at[k], pass_recv.at[k], mate, rep)

    each(1, planes, lambda k: own(k).start())
    first = remote(x_ref, out_ref.at[me], pass_send.at[0], pass_recv.at[0], mate, rep)
    first.start()
    out_ref[me] = x_ref[...]

    def hand_on(k):
        own(k).wait_recv()
        passed(k).start()

    each(1, planes, hand_on)
    first.wait()

    def finish(k):
        own(k).wait_send()
        passed(k).wait()

    each(1, planes, finish)


def gather(x_src):
    panels = lax.axis_size("panel")
    sems = pltpu.SemaphoreType.DMA((panels // 2,))
    vmem = pl.BlockSpec(memory_space=pltpu.VMEM)
    out = pl.pallas_call(
        gather_kernel,
        out_shape=jax.ShapeDtypeStruct((panels,) + x_src.shape, x_src.dtype),
        in_specs=[vmem],
        out_specs=vmem,
        scratch_shapes=[sems] * 4,
        compiler_params=pltpu.CompilerParams(collective_id=0, has_side_effects=True),
    )(x_src)
    return out.reshape(panels * x_src.shape[0], x_src.shape[1])


def reduce_kernel(
    part_ref, att_ref, grad_src_ref, grad_weight_ref, att_src_ref, att_dst_ref,
    mate_part, mate_att, merged, landed, chunks, chunk, mate_sems, send, recv, row_send, row_recv,
    chunk_send, chunk_recv,
):
    plane, core, rep, planes, reps = place()
    owners, rows = merged.shape[:2]
    share = rows - 2 * CHUNK
    devices = 2 * owners
    me = plane * reps + rep
    panel = plane * 2 + core
    mate = plane * 2 + 1 - core
    index = panel * reps + rep
    barrier = pltpu.get_barrier_semaphore()

    def other(k):
        e = lax.rem(index + k, devices)
        return e // reps, lax.rem(e, reps)

    def greet(k):
        pl.semaphore_signal(barrier, inc=1, device_id=other(k), device_id_type=MESH)

    each(1, devices, greet)
    pl.semaphore_wait(barrier, devices - 1)

    swap = remote(part_ref.at[1 - core], mate_part, mate_sems.at[0], mate_sems.at[1], mate, rep)
    swap_att = remote(att_ref, mate_att, mate_sems.at[2], mate_sems.at[3], mate, rep)
    swap.start()
    swap_att.start()
    swap_att.wait()
    pair_att = att_ref[...].astype(F32) + mate_att[...].astype(F32)
    pair_att = pair_att[: CHUNK // 2] + pair_att[CHUNK // 2 :]
    top = pair_att.astype(BF16).astype(F32)
    tail = jnp.concatenate([top, pair_att - top], axis=0).astype(BF16)
    swap.wait()

    def to_owner(k):
        d = lax.rem(me + k, owners)
        return remote(
            merged.at[d], landed.at[k], send.at[k], recv.at[k], d // reps * 2 + core, lax.rem(d, reps)
        )

    def merge(k):
        d = lax.rem(me + k, owners)
        summed = part_ref[core, d].astype(F32) + mate_part[d].astype(F32)
        merged[d, : share + CHUNK, :] = summed.astype(BF16)
        merged[d, share + CHUNK :, :] = tail

    def merge_send(k):
        merge(k)
        to_owner(k).start()

    each(1, owners, merge_send)
    merge(0)

    def collect(k, total):
        to_owner(k).wait_recv()
        return total + landed[k].astype(F32)

    total = lax.fori_loop(1, owners, collect, merged[me].astype(F32))

    chunk[...] = total[share : share + CHUNK].astype(BF16)

    def spread(k):
        e_panel, e_rep = other(k)
        return remote(chunk, chunks.at[index], chunk_send.at[k], chunk_recv.at[k], e_panel, e_rep)

    def rows_to(k):
        part = grad_src_ref.at[pl.ds(pl.multiple_of(rep * share, share), share)]
        return remote(part, part, row_send.at[k], row_recv.at[k], panel, lax.rem(rep + k, reps))

    grad_src_ref[pl.ds(pl.multiple_of(rep * share, share), share), :] = total[:share]
    each(1, devices, lambda k: spread(k).start())
    each(1, reps, lambda k: rows_to(k).start())
    chunks[index] = chunk[...]
    att = total[share + CHUNK :]
    att = att[: CHUNK // 2] + att[CHUNK // 2 :]
    heads, head_dim = att_src_ref.shape
    per = LANES // head_dim
    lines = [
        att[r : r + 1, q * head_dim : (q + 1) * head_dim] for r in range(2 * heads // per) for q in range(per)
    ]
    att_src_ref[...] = jnp.concatenate(lines[:heads], axis=0)
    att_dst_ref[...] = jnp.concatenate(lines[heads:], axis=0)
    each(1, owners, lambda k: to_owner(k).wait_send())
    each(1, devices, lambda k: spread(k).wait())
    each(1, reps, lambda k: rows_to(k).wait())
    inputs, width = grad_weight_ref.shape
    half = inputs * width // LANES // CHUNK // 2
    for n in range(2 * half):
        c, d = n // half, n % half
        sender = (d // reps * 2 + c) * reps + d % reps
        at, col = n * CHUNK % inputs, n * CHUNK // inputs * LANES
        grad_weight_ref[at : at + CHUNK, col : col + LANES] = chunks[sender].astype(F32)


def reduce(part, part_att, inputs, width, heads, rows):
    owners, lines = part.shape[1:3]
    reps = lax.axis_size("rep")
    vmem = pl.BlockSpec(memory_space=pltpu.VMEM)
    dma = pltpu.SemaphoreType.DMA
    return pl.pallas_call(
        reduce_kernel,
        out_shape=(
            jax.ShapeDtypeStruct((rows, inputs), F32),
            jax.ShapeDtypeStruct((inputs, width), F32),
            jax.ShapeDtypeStruct((heads, width // heads), F32),
            jax.ShapeDtypeStruct((heads, width // heads), F32),
        ),
        in_specs=[vmem] * 2,
        out_specs=(vmem,) * 4,
        scratch_shapes=[
            pltpu.VMEM((owners, lines, LANES), BF16),
            pltpu.VMEM((CHUNK, LANES), BF16),
            pltpu.VMEM((owners, lines + CHUNK, LANES), BF16),
            pltpu.VMEM((owners, lines + CHUNK, LANES), BF16),
            pltpu.VMEM((2 * owners, CHUNK, LANES), BF16),
            pltpu.VMEM((CHUNK, LANES), BF16),
            dma((4,)),
            dma((owners,)),
            dma((owners,)),
            dma((reps,)),
            dma((reps,)),
            dma((2 * owners,)),
            dma((2 * owners,)),
        ],
        compiler_params=pltpu.CompilerParams(
            collective_id=1, has_side_effects=True, vmem_limit_bytes=62 * 1024 * 1024
        ),
    )(part, part_att)


def layer(x_all, x_dst, weight, att_src, att_dst, grad_out, rows, cols, masks, counts):
    heads = att_src.shape[0]
    inputs, width = weight.shape
    slots, blk = masks.shape[:2]
    sources, dest = x_all.shape[0], x_dst.shape[0]
    blocks = sources // blk
    reps = lax.axis_size("rep")
    owners = blocks // 2 * reps
    vmem = pl.BlockSpec(memory_space=pltpu.VMEM)
    smem = pl.BlockSpec(memory_space=pltpu.SMEM)
    return pl.pallas_call(
        layer_kernel,
        out_shape=(
            jax.ShapeDtypeStruct((dest, inputs), F32),
            jax.ShapeDtypeStruct((2, owners, blk // reps + CHUNK, LANES), BF16),
            jax.ShapeDtypeStruct((CHUNK, LANES), BF16),
        ),
        in_specs=[smem] * 3 + [vmem] * 7,
        out_specs=(vmem,) * 3,
        scratch_shapes=[
            pltpu.VMEM((sources, width), BF16),
            pltpu.VMEM((blocks, width, blk), BF16),
            pltpu.VMEM((dest, width), BF16),
            pltpu.VMEM((dest // blk, width, blk), BF16),
            pltpu.VMEM((blocks, heads, blk), F32),
            pltpu.VMEM((heads, dest, LANES), F32),
            pltpu.VMEM((heads, dest, LANES), F32),
            pltpu.VMEM((slots, heads, blk, blk), F32),
            pltpu.VMEM((slots, heads, blk, blk), F32),
            pltpu.VMEM((dest, width), F32),
            pltpu.VMEM((dest, LANES), F32),
            pltpu.VMEM((dest, LANES), BF16),
            pltpu.VMEM((blocks, width, blk), F32),
            pltpu.VMEM((blocks, heads, blk), F32),
            pltpu.VMEM((heads, dest, LANES), F32),
            pltpu.VMEM((width, sources), BF16),
        ],
        compiler_params=pltpu.CompilerParams(vmem_limit_bytes=62 * 1024 * 1024),
    )(rows, cols, counts, x_all, x_dst, weight, att_src, att_dst, grad_out, masks)


def shards(
    x_src, x_dst, weight, att_src, att_dst, grad_out, block_rows, block_cols, block_masks, block_counts
):
    x_all = gather(x_src)
    grad_dst, part, part_att = layer(
        x_all, x_dst, weight, att_src, att_dst, grad_out, block_rows, block_cols, block_masks, block_counts
    )
    grad_src, grad_weight, grad_att_src, grad_att_dst = reduce(
        part, part_att, weight.shape[0], weight.shape[1], att_src.shape[0], x_src.shape[0]
    )
    return grad_src, grad_dst, grad_weight, grad_att_src, grad_att_dst


def solution(mesh):
    both = P(("panel", "rep"))
    return jax.shard_map(
        shards,
        mesh=mesh,
        in_specs=(P("panel", None), both, P(), P(), P(), both, both, both, both, both),
        out_specs=(P("panel", None), both, P(), P(), P()),
        check_vma=False,
    )
```

```python
import functools

import jax
import jax.numpy as jnp
from jax import lax
from jax.experimental import pallas as pl
from jax.experimental.pallas import tpu as pltpu
from jax.sharding import PartitionSpec as P

F32 = jnp.float32
BF16 = jnp.bfloat16
MESH = pl.DeviceIdType.MESH
LANES = 128
CHUNK = 16
LOG2_E = 1.4426950408889634


def mm(a, b, ca=1, cb=0):
    return lax.dot_general(a, b, (((ca,), (cb,)), ((), ())), preferred_element_type=F32)


def split(values, parts):
    pieces = []
    for _ in range(parts):
        piece = values.astype(BF16)
        pieces.append(piece)
        values = values - piece.astype(F32)
    return pieces


def mm_split(a, b, parts, ca=1, cb=0):
    return sum(mm(piece, b, ca, cb) for piece in split(a, parts))


def edge_terms(pre):
    grown = 1.0 + jnp.exp2(-jnp.abs(pre))
    sigma = jnp.maximum(pre, 0.2 * pre) + 0.8 * jnp.log2(grown)
    return jnp.exp2(sigma), 0.6 + 0.4 * jnp.tanh((0.5 / LOG2_E) * pre)


def iota(shape, dim):
    return lax.broadcasted_iota(jnp.int32, shape, dim)


def layer_kernel(
    rows_ref, cols_ref, count_ref, x_all_ref, x_dst_ref, weight_ref, att_src_ref, att_dst_ref,
    grad_ref, masks_ref,
    grad_dst_ref, part_ref, part_att_ref,
    proj_src, proj_turned, proj_dst, cotan_turned, score_src, score_wide, inv_wide, weights, slopes,
    numer, denom, centre, grad_source, grad_score_src, grad_score_dst, source,
):
    heads, head_dim = att_src_ref.shape
    width = weight_ref.shape[1]
    pairs = width // LANES
    blk = masks_ref.shape[1]
    source_blocks = x_all_ref.shape[0] // blk
    dest = x_dst_ref.shape[0]
    count = count_ref[0]
    owners, share = part_ref.shape[1], part_ref.shape[2] - CHUNK
    reps = x_all_ref.shape[0] // source_blocks // share
    inputs = weight_ref.shape[0]

    lane_head = iota((heads, width), 1) // head_dim
    own = lane_head == iota((heads, width), 0)
    spread_src = jnp.where(own, jnp.concatenate([att_src_ref[...]] * heads, axis=1), 0.0)
    spread_dst = jnp.where(own, jnp.concatenate([att_dst_ref[...]] * heads, axis=1), 0.0)
    pad_rows = jnp.zeros((LANES - heads, width), F32)
    row = iota((LANES, width), 0)
    ones_heads = jnp.where(
        (lax.rem(row, heads) == iota((LANES, width), 1) // head_dim) & (row < 2 * heads), 1.0, 0.0
    ).astype(BF16)
    ones_turned = jnp.where(
        iota((width, LANES), 0) // head_dim == iota((width, LANES), 1), 1.0, 0.0
    ).astype(BF16)
    tall = jnp.concatenate([spread_src, spread_dst, pad_rows[heads:]], axis=0).astype(BF16)

    stack_src = jnp.concatenate([p.astype(F32) for p in split(spread_src, 3)], axis=0)
    stack_dst = jnp.concatenate([p.astype(F32) for p in split(spread_dst, 3)], axis=0)
    stacked = stack_src.astype(BF16)
    weight_turned = weight_ref[...].T
    proj_src[...] = mm(x_all_ref[...], weight_ref[...]).astype(BF16)
    per = min(4, source_blocks)
    for s in range(0, source_blocks, per):
        turned = mm(weight_turned, x_all_ref[s * blk : (s + per) * blk, :], 1, 1).astype(BF16)
        got = mm(stacked, turned)
        got = (got[:heads] + got[heads : 2 * heads] + got[2 * heads :]) * LOG2_E
        for n in range(per):
            proj_turned[s + n] = turned[:, n * blk : (n + 1) * blk]
            score_src[s + n] = got[:, n * blk : (n + 1) * blk]
    proj_dst[...] = mm(x_dst_ref[...], weight_ref[...]).astype(BF16)
    stacked = jnp.concatenate(
        [stack_dst, stack_src, jnp.zeros((LANES - 6 * heads, width), F32)], axis=0
    ).astype(BF16)
    got = mm(proj_dst[...], stacked, 1, 1) * LOG2_E
    shift = [got] + [pltpu.roll(got, LANES - n * heads, 1) for n in range(1, 6)]
    score_d = shift[0] + shift[1] + shift[2]
    pre_self = score_d + (shift[3] + shift[4] + shift[5])
    for h in range(heads):
        score_wide[h] = jnp.broadcast_to(score_d[:, h : h + 1], (dest, LANES))
    for d in range(dest // blk):
        cotan_turned[d] = grad_ref[d * blk : (d + 1) * blk, :].T

    numer[...] = jnp.zeros_like(numer)
    denom[...] = jnp.zeros_like(denom)
    grad_source[...] = jnp.zeros_like(grad_source)
    grad_score_src[...] = jnp.zeros_like(grad_score_src)
    grad_score_dst[...] = jnp.zeros_like(grad_score_dst)

    low = (iota((1, LANES), 1) < head_dim).astype(F32).astype(BF16)
    high = (iota((1, LANES), 1) >= head_dim).astype(F32).astype(BF16)
    second = iota((2 * blk, LANES), 0) // blk
    lane = iota((2 * blk, LANES), 1)

    def both(values):
        return jnp.concatenate([values * low, values * high], axis=0)

    ones_pair = [jnp.where(lane == 2 * g + second, 1.0, 0.0).astype(BF16) for g in range(pairs)]
    column = iota((LANES, 2 * blk), 0)
    column_head = iota((LANES, 2 * blk), 1) // blk
    minus_pair = [
        jnp.where(lax.rem(column, heads) == 2 * g + column_head, -1.0, 0.0) for g in range(pairs)
    ]
    minus_pair = [jnp.where(column < 2 * heads, m, 0.0).astype(BF16) for m in minus_pair]

    def forward(b, carry):
        r = pl.ds(pl.multiple_of(rows_ref[b] * blk, blk), blk)
        c = cols_ref[b]
        src = pl.ds(pl.multiple_of(c * blk, blk), blk)
        live = masks_ref[b] > 0
        scores = score_src[c]
        for g in range(pairs):
            at = slice(g * LANES, (g + 1) * LANES)
            found = []
            for h in (2 * g, 2 * g + 1):
                edge, slope = edge_terms(score_wide[h, r, :] + scores[h : h + 1, :])
                edge = jnp.where(live, edge, 0.0)
                weights[b, h] = edge
                slopes[b, h] = slope
                found.append(edge.astype(BF16))
            right = jnp.concatenate(
                [both(proj_src[src, at]), ones_pair[g]], axis=1
            )
            got = mm(jnp.concatenate(found, axis=1), right)
            numer[r, at] += got[:, :LANES]
            denom[r, :] += got[:, LANES:]
        return carry

    lax.fori_loop(0, count, forward, 0)

    lanes = iota((dest, LANES), 1)

    def two_pieces(values):
        top = values.astype(BF16).astype(F32)
        return (top + pltpu.roll(values - top, heads, 1)).astype(BF16)

    def over_heads(values):
        return jnp.where(lanes < heads, values, 0.0)

    feats = proj_dst[...].astype(F32)
    cotan = grad_ref[...].astype(F32)
    self_weight, self_slope = edge_terms(pre_self)
    self_weight = over_heads(self_weight)
    inverse = 1.0 / (denom[...] + jnp.where(lanes < heads, self_weight, 1.0))
    total = numer[...] + mm(two_pieces(self_weight), ones_heads) * feats
    attended = total * mm(two_pieces(over_heads(inverse)), ones_heads)
    narrow = over_heads(mm_split(cotan * attended, ones_turned, 2))
    centre[...] = two_pieces(narrow)
    self_att = self_weight * inverse
    self_pair = mm_split(cotan * feats, ones_turned, 2)
    self_grad = self_att * (self_pair - narrow) * self_slope
    for h in range(heads):
        inv_wide[h] = jnp.broadcast_to(inverse[:, h : h + 1], (dest, LANES))

    def backward(b, carry):
        d = rows_ref[b]
        r = pl.ds(pl.multiple_of(d * blk, blk), blk)
        c = cols_ref[b]
        nothing = jnp.zeros((head_dim, blk), BF16)
        for g in range(pairs):
            at = slice(g * LANES, (g + 1) * LANES)
            left = jnp.concatenate([grad_ref[r, at], centre[r, :]], axis=1)
            feats_turned = proj_turned[c, at, :]
            right = jnp.concatenate(
                [
                    jnp.concatenate([feats_turned[:head_dim], nothing], axis=1),
                    jnp.concatenate([nothing, feats_turned[head_dim:]], axis=1),
                    minus_pair[g],
                ],
                axis=0,
            )
            apart = mm(left, right)
            shares, sums = [], []
            for q in range(2):
                h = 2 * g + q
                share = weights[b, h] * inv_wide[h, r, :]
                grad = share * apart[:, q * blk : (q + 1) * blk] * slopes[b, h]
                sums.append(jnp.sum(grad, axis=0, keepdims=True))
                grad_score_dst[h, r, :] += grad
                shares.append(share.astype(BF16))
            grad_score_src[c, 2 * g : 2 * g + 2, :] += jnp.concatenate(sums, axis=0)
            got = mm(cotan_turned[d, at, :], jnp.concatenate(shares, axis=1))
            grad_source[c, at, :] += jnp.concatenate(
                [got[:head_dim, :blk], got[head_dim:, blk:]], axis=0
            )
        return carry

    lax.fori_loop(0, count, backward, 0)

    score_grad = self_grad
    for h in range(heads):
        score_grad += jnp.where(lanes == h, jnp.sum(grad_score_dst[h], axis=1, keepdims=True), 0.0)
    grads = (self_grad + pltpu.roll(score_grad, heads, 1)).astype(BF16)
    flat = (mm(two_pieces(self_att), ones_heads) * cotan + mm(grads, tall)).astype(BF16)
    grad_dst_ref[...] = mm(flat, weight_ref[...], 1, 1)
    part_weight = mm(x_dst_ref[...], flat, 0, 0)
    att_part = mm(grads, proj_dst[...], 0, 0)

    scores = jnp.concatenate([grad_score_src[s] for s in range(source_blocks)], axis=1).astype(BF16)
    spread_turned = spread_src.T.astype(BF16)
    for s in range(source_blocks):
        at = slice(s * blk, (s + 1) * blk)
        source[:, at] = (grad_source[s] + mm(spread_turned, scores[:, at])).astype(BF16)
    weight_turned_part = mm(source[...], x_all_ref[...])
    att_src_part = att_part[:heads] + mm(scores, proj_src[...])
    att_dst_part = att_part[heads : 2 * heads]
    for s in range(0, source_blocks, per):
        product = mm(weight_ref[...], source[:, s * blk : (s + per) * blk])
        for n in range(s, s + per):
            block = product[:, (n - s) * blk : (n - s + 1) * blk].T.astype(part_ref.dtype)
            for rep in range(reps):
                part_ref[n % 2, n // 2 * reps + rep, :share, :] = block[rep * share : (rep + 1) * share]
    part_weight += weight_turned_part.T
    tiles = [
        part_weight[n : n + CHUNK, g * LANES : (g + 1) * LANES].astype(part_ref.dtype)
        for g in range(pairs)
        for n in range(0, inputs, CHUNK)
    ]
    half = len(tiles) // 2
    for core in range(2):
        for owner in range(owners):
            part_ref[core, owner, share:, :] = (
                tiles[core * half + owner] if owner < half else jnp.zeros((CHUNK, LANES), part_ref.dtype)
            )
    src_row = jnp.sum(jnp.where(own, att_src_part, 0.0), axis=0, keepdims=True)
    dst_row = jnp.sum(jnp.where(own, att_dst_part, 0.0), axis=0, keepdims=True)
    stack = [row[:, g * LANES : (g + 1) * LANES] for row in (src_row, dst_row) for g in range(pairs)]
    att = jnp.concatenate(stack, axis=0)
    part_att_ref[...] = jnp.concatenate(
        [att.astype(BF16).astype(F32), att - att.astype(BF16).astype(F32)], axis=0
    ).astype(part_att_ref.dtype)


def place():
    panel, rep = lax.axis_index("panel"), lax.axis_index("rep")
    return panel // 2, panel % 2, rep, lax.axis_size("panel") // 2, lax.axis_size("rep")


def remote(src, dst, send, recv, panel, rep):
    return pltpu.make_async_remote_copy(
        src_ref=src, dst_ref=dst, send_sem=send, recv_sem=recv, device_id=(panel, rep), device_id_type=MESH
    )


def each(start, stop, step):
    def body(k, carry):
        step(k)
        return carry

    lax.fori_loop(start, stop, body, 0)


def gather_kernel(x_ref, out_ref, send, recv, pass_send, pass_recv):
    plane, core, rep, planes, _ = place()
    me = plane * 2 + core
    mate = plane * 2 + 1 - core
    barrier = pltpu.get_barrier_semaphore()

    def peer(k):
        return lax.rem(plane + k, planes) * 2 + core

    def greet(k):
        pl.semaphore_signal(barrier, inc=1, device_id=(peer(k), rep), device_id_type=MESH)

    each(1, planes, greet)
    pl.semaphore_signal(barrier, inc=1, device_id=(mate, rep), device_id_type=MESH)
    pl.semaphore_wait(barrier, planes)

    def own(k):
        return remote(x_ref, out_ref.at[me], send.at[k], recv.at[k], peer(k), rep)

    def passed(k):
        slot = lax.rem(plane + planes - k, planes) * 2 + core
        return remote(out_ref.at[slot], out_ref.at[slot], pass_send.at[k], pass_recv.at[k], mate, rep)

    each(1, planes, lambda k: own(k).start())
    first = remote(x_ref, out_ref.at[me], pass_send.at[0], pass_recv.at[0], mate, rep)
    first.start()
    out_ref[me] = x_ref[...]

    def hand_on(k):
        own(k).wait_recv()
        passed(k).start()

    each(1, planes, hand_on)
    first.wait()

    def finish(k):
        own(k).wait_send()
        passed(k).wait()

    each(1, planes, finish)


def gather(x_src):
    panels = lax.axis_size("panel")
    sems = pltpu.SemaphoreType.DMA((panels // 2,))
    vmem = pl.BlockSpec(memory_space=pltpu.VMEM)
    out = pl.pallas_call(
        gather_kernel,
        out_shape=jax.ShapeDtypeStruct((panels,) + x_src.shape, x_src.dtype),
        in_specs=[vmem],
        out_specs=vmem,
        scratch_shapes=[sems] * 4,
        compiler_params=pltpu.CompilerParams(collective_id=0, has_side_effects=True),
    )(x_src)
    return out.reshape(panels * x_src.shape[0], x_src.shape[1])


def reduce_kernel(
    part_ref, att_ref, rows_ref, chunks, att_out_ref,
    mate_part, mate_att, merged, landed, chunk, tail, att_landed, mate_sems, swap_send, swap_recv,
    send, recv, row_send, row_recv, chunk_send, chunk_recv, att_send, att_recv, sum_send, sum_recv,
):
    plane, core, rep, planes, reps = place()
    owners, rows = merged.shape[:2]
    share = rows - CHUNK
    devices = 2 * owners
    me = plane * reps + rep
    panel = plane * 2 + core
    mate = plane * 2 + 1 - core
    index = panel * reps + rep
    barrier = pltpu.get_barrier_semaphore()

    def other(k):
        e = lax.rem(index + k, devices)
        return e // reps, lax.rem(e, reps)

    def greet(k):
        pl.semaphore_signal(barrier, inc=1, device_id=other(k), device_id_type=MESH)

    each(1, devices, greet)
    pl.semaphore_wait(barrier, devices - 1)

    pieces = swap_send.shape[0]
    span = owners // pieces

    def piece_at(n):
        return lax.rem(me // span + 1 + n, pieces)

    def swap(n):
        n = piece_at(n)
        piece = pl.ds(n * span, span)
        return remote(
            part_ref.at[1 - core, piece], mate_part.at[piece], swap_send.at[n], swap_recv.at[n], mate, rep
        )

    swap_att = remote(att_ref, mate_att, mate_sems.at[0], mate_sems.at[1], mate, rep)
    each(0, pieces, lambda n: swap(n).start())
    swap_att.start()

    def to_owner(d):
        slot = lax.rem(me - d + owners, owners)
        return remote(
            merged.at[d], landed.at[slot], send.at[d], recv.at[slot], d // reps * 2 + core, lax.rem(d, reps)
        )

    def from_owner(k):
        return remote(merged.at[0], landed.at[k], send.at[0], recv.at[k], mate, rep)

    def merge_piece(n):
        swap(n).wait_recv()

        def merge_send(j):
            d = piece_at(n) * span + lax.rem(me + j, span)
            summed = part_ref[core, d].astype(F32) + mate_part[d].astype(F32)
            merged[d] = summed.astype(BF16)

            @pl.when(d != me)
            def _():
                to_owner(d).start()

        each(0, span, merge_send)

    each(0, pieces, merge_piece)

    swap_att.wait()
    pair_att = att_ref[...].astype(F32) + mate_att[...].astype(F32)

    def as_pieces(pair):
        folded = pair[: CHUNK // 2] + pair[CHUNK // 2 :]
        top = folded.astype(BF16).astype(F32)
        return jnp.concatenate([top, folded - top], axis=0)

    tail[...] = as_pieces(pair_att).astype(BF16)

    def att_to_first(k):
        return remote(tail, att_landed.at[k], att_send.at[0], att_recv.at[k], core, 0)

    @pl.when(me != 0)
    def _():
        att_to_first(me).start()

    def collect(k, total):
        from_owner(k).wait_recv()
        return total + landed[k].astype(F32)

    total = lax.fori_loop(1, owners, collect, merged[me].astype(F32))

    chunk[...] = total[share:].astype(BF16)

    def spread(k):
        e_panel, e_rep = other(k)
        return remote(chunk, chunks.at[index], chunk_send.at[k], chunk_recv.at[k], e_panel, e_rep)

    def rows_to(k):
        part = rows_ref.at[pl.ds(pl.multiple_of(rep * share, share), share)]
        return remote(part, part, row_send.at[k], row_recv.at[k], panel, lax.rem(rep + k, reps))

    rows_ref[pl.ds(pl.multiple_of(rep * share, share), share), :] = total[:share]
    each(1, devices, lambda k: spread(k).start())
    each(1, reps, lambda k: rows_to(k).start())
    chunks[index] = chunk[...]

    def sum_to(k):
        return remote(
            att_out_ref, att_out_ref, sum_send.at[k], sum_recv.at[0], k // reps * 2 + core, lax.rem(k, reps)
        )

    @pl.when(me == 0)
    def _():
        def add_att(k, found):
            att_to_first(k).wait_recv()
            return found + att_landed[k].astype(F32)

        found = lax.fori_loop(1, owners, add_att, tail[...].astype(F32))
        att_out_ref[...] = as_pieces(found).astype(BF16)
        each(1, owners, lambda k: sum_to(k).start())
        each(1, owners, lambda k: sum_to(k).wait_send())

    @pl.when(me != 0)
    def _():
        att_to_first(me).wait_send()
        sum_to(me).wait_recv()

    each(0, pieces, lambda n: swap(n).wait_send())

    def sent(d):
        @pl.when(d != me)
        def _():
            to_owner(d).wait_send()

    each(0, owners, sent)
    each(1, devices, lambda k: spread(k).wait())
    each(1, reps, lambda k: rows_to(k).wait())


def unpack_kernel(reps, rows_ref, chunks, att_ref, grad_src_ref, grad_weight_ref, att_src_ref, att_dst_ref):
    grad_src_ref[...] = rows_ref[...]
    att = att_ref[...].astype(F32)
    att = att[: CHUNK // 2] + att[CHUNK // 2 :]
    heads, head_dim = att_src_ref.shape
    per = LANES // head_dim
    lines = [
        att[r : r + 1, q * head_dim : (q + 1) * head_dim] for r in range(2 * heads // per) for q in range(per)
    ]
    att_src_ref[...] = jnp.concatenate(lines[:heads], axis=0)
    att_dst_ref[...] = jnp.concatenate(lines[heads:], axis=0)
    inputs, width = grad_weight_ref.shape
    half = inputs * width // LANES // CHUNK // 2
    for n in range(2 * half):
        c, d = n // half, n % half
        sender = (d // reps * 2 + c) * reps + d % reps
        at, col = n * CHUNK % inputs, n * CHUNK // inputs * LANES
        grad_weight_ref[at : at + CHUNK, col : col + LANES] = chunks[sender].astype(F32)


def reduce(part, part_att, inputs, width, heads, rows):
    owners, lines = part.shape[1:3]
    reps = lax.axis_size("rep")
    pieces = 4
    vmem = pl.BlockSpec(memory_space=pltpu.VMEM)
    dma = pltpu.SemaphoreType.DMA
    packed = pl.pallas_call(
        reduce_kernel,
        out_shape=(
            jax.ShapeDtypeStruct((rows, inputs), F32),
            jax.ShapeDtypeStruct((2 * owners, CHUNK, LANES), BF16),
            jax.ShapeDtypeStruct((CHUNK, LANES), BF16),
        ),
        in_specs=[vmem] * 2,
        out_specs=(vmem,) * 3,
        scratch_shapes=[
            pltpu.VMEM((owners, lines, LANES), BF16),
            pltpu.VMEM((CHUNK, LANES), BF16),
            pltpu.VMEM((owners, lines, LANES), BF16),
            pltpu.VMEM((owners, lines, LANES), BF16),
            pltpu.VMEM((CHUNK, LANES), BF16),
            pltpu.VMEM((CHUNK, LANES), BF16),
            pltpu.VMEM((owners, CHUNK, LANES), BF16),
            dma((2,)),
            dma((pieces,)),
            dma((pieces,)),
            dma((owners,)),
            dma((owners,)),
            dma((reps,)),
            dma((reps,)),
            dma((2 * owners,)),
            dma((2 * owners,)),
            dma((1,)),
            dma((owners,)),
            dma((owners,)),
            dma((1,)),
        ],
        compiler_params=pltpu.CompilerParams(
            collective_id=1, has_side_effects=True, vmem_limit_bytes=32 * 1024 * 1024
        ),
    )(part, part_att)
    return pl.pallas_call(
        functools.partial(unpack_kernel, reps),
        out_shape=(
            jax.ShapeDtypeStruct((rows, inputs), F32),
            jax.ShapeDtypeStruct((inputs, width), F32),
            jax.ShapeDtypeStruct((heads, width // heads), F32),
            jax.ShapeDtypeStruct((heads, width // heads), F32),
        ),
        in_specs=[vmem] * 3,
        out_specs=(vmem,) * 4,
    )(*packed)


def layer(x_all, x_dst, weight, att_src, att_dst, grad_out, rows, cols, masks, counts):
    heads = att_src.shape[0]
    inputs, width = weight.shape
    slots, blk = masks.shape[:2]
    sources, dest = x_all.shape[0], x_dst.shape[0]
    blocks = sources // blk
    reps = lax.axis_size("rep")
    owners = blocks // 2 * reps
    vmem = pl.BlockSpec(memory_space=pltpu.VMEM)
    smem = pl.BlockSpec(memory_space=pltpu.SMEM)
    return pl.pallas_call(
        layer_kernel,
        out_shape=(
            jax.ShapeDtypeStruct((dest, inputs), F32),
            jax.ShapeDtypeStruct((2, owners, blk // reps + CHUNK, LANES), BF16),
            jax.ShapeDtypeStruct((CHUNK, LANES), BF16),
        ),
        in_specs=[smem] * 3 + [vmem] * 7,
        out_specs=(vmem,) * 3,
        scratch_shapes=[
            pltpu.VMEM((sources, width), BF16),
            pltpu.VMEM((blocks, width, blk), BF16),
            pltpu.VMEM((dest, width), BF16),
            pltpu.VMEM((dest // blk, width, blk), BF16),
            pltpu.VMEM((blocks, heads, blk), F32),
            pltpu.VMEM((heads, dest, LANES), F32),
            pltpu.VMEM((heads, dest, LANES), F32),
            pltpu.VMEM((slots, heads, blk, blk), F32),
            pltpu.VMEM((slots, heads, blk, blk), F32),
            pltpu.VMEM((dest, width), F32),
            pltpu.VMEM((dest, LANES), F32),
            pltpu.VMEM((dest, LANES), BF16),
            pltpu.VMEM((blocks, width, blk), F32),
            pltpu.VMEM((blocks, heads, blk), F32),
            pltpu.VMEM((heads, dest, LANES), F32),
            pltpu.VMEM((width, sources), BF16),
        ],
        compiler_params=pltpu.CompilerParams(vmem_limit_bytes=62 * 1024 * 1024),
    )(rows, cols, counts, x_all, x_dst, weight, att_src, att_dst, grad_out, masks)


def shards(
    x_src, x_dst, weight, att_src, att_dst, grad_out, block_rows, block_cols, block_masks, block_counts
):
    x_all = gather(x_src)
    grad_dst, part, part_att = layer(
        x_all, x_dst, weight, att_src, att_dst, grad_out, block_rows, block_cols, block_masks, block_counts
    )
    grad_src, grad_weight, grad_att_src, grad_att_dst = reduce(
        part, part_att, weight.shape[0], weight.shape[1], att_src.shape[0], x_src.shape[0]
    )
    return grad_src, grad_dst, grad_weight, grad_att_src, grad_att_dst


def solution(mesh):
    both = P(("panel", "rep"))
    return jax.shard_map(
        shards,
        mesh=mesh,
        in_specs=(P("panel", None), both, P(), P(), P(), both, both, both, both, both),
        out_specs=(P("panel", None), both, P(), P(), P()),
        check_vma=False,
    )
```

```python
import functools

import jax
import jax.numpy as jnp
from jax import lax
from jax.experimental import pallas as pl
from jax.experimental.pallas import tpu as pltpu
from jax.sharding import PartitionSpec as P

F32 = jnp.float32
BF16 = jnp.bfloat16
MESH = pl.DeviceIdType.MESH
LANES = 128
CHUNK = 16
LOG2_E = 1.4426950408889634


def mm(a, b, ca=1, cb=0):
    return lax.dot_general(a, b, (((ca,), (cb,)), ((), ())), preferred_element_type=F32)


def split(values, parts):
    pieces = []
    for _ in range(parts):
        piece = values.astype(BF16)
        pieces.append(piece)
        values = values - piece.astype(F32)
    return pieces


def mm_split(a, b, parts, ca=1, cb=0):
    return sum(mm(piece, b, ca, cb) for piece in split(a, parts))


def edge_terms(pre):
    grown = 1.0 + jnp.exp2(-jnp.abs(pre))
    sigma = jnp.maximum(pre, 0.2 * pre) + 0.8 * jnp.log2(grown)
    return jnp.exp2(sigma), 0.6 + 0.4 * jnp.tanh((0.5 / LOG2_E) * pre)


def iota(shape, dim):
    return lax.broadcasted_iota(jnp.int32, shape, dim)


def layer_kernel(
    rows_ref, cols_ref, count_ref, x_all_ref, x_dst_ref, weight_ref, att_src_ref, att_dst_ref,
    grad_hbm, masks_hbm,
    grad_dst_ref, part_ref, part_att_ref,
    proj_src, proj_turned, proj_dst, cotan_turned, score_src, score_wide, inv_wide, weights, slopes,
    numer, denom, centre, grad_source, grad_score_src, grad_score_dst, source,
    grad_ref, masks_ref, load_sems,
):
    heads, head_dim = att_src_ref.shape
    width = weight_ref.shape[1]
    pairs = width // LANES
    blk = masks_ref.shape[1]
    source_blocks = x_all_ref.shape[0] // blk
    dest = x_dst_ref.shape[0]
    count = count_ref[0]
    owners, share = part_ref.shape[1], part_ref.shape[2] - CHUNK
    reps = x_all_ref.shape[0] // source_blocks // share
    inputs = weight_ref.shape[0]

    load_grad = pltpu.make_async_copy(grad_hbm, grad_ref, load_sems.at[0])
    load_masks = pltpu.make_async_copy(masks_hbm, masks_ref, load_sems.at[1])
    load_grad.start()
    load_masks.start()

    lane_head = iota((heads, width), 1) // head_dim
    own = lane_head == iota((heads, width), 0)
    spread_src = jnp.where(own, jnp.concatenate([att_src_ref[...]] * heads, axis=1), 0.0)
    spread_dst = jnp.where(own, jnp.concatenate([att_dst_ref[...]] * heads, axis=1), 0.0)
    pad_rows = jnp.zeros((LANES - heads, width), F32)
    row = iota((LANES, width), 0)
    ones_heads = jnp.where(
        (lax.rem(row, heads) == iota((LANES, width), 1) // head_dim) & (row < 2 * heads), 1.0, 0.0
    ).astype(BF16)
    ones_turned = jnp.where(
        iota((width, LANES), 0) // head_dim == iota((width, LANES), 1), 1.0, 0.0
    ).astype(BF16)
    tall = jnp.concatenate([spread_src, spread_dst, pad_rows[heads:]], axis=0).astype(BF16)

    stack_src = jnp.concatenate([p.astype(F32) for p in split(spread_src, 3)], axis=0)
    stack_dst = jnp.concatenate([p.astype(F32) for p in split(spread_dst, 3)], axis=0)
    stacked = stack_src.astype(BF16)
    weight_turned = weight_ref[...].T
    proj_src[...] = mm(x_all_ref[...], weight_ref[...]).astype(BF16)
    per = min(4, source_blocks)
    for s in range(0, source_blocks, per):
        turned = mm(weight_turned, x_all_ref[s * blk : (s + per) * blk, :], 1, 1).astype(BF16)
        got = mm(stacked, turned)
        got = (got[:heads] + got[heads : 2 * heads] + got[2 * heads :]) * LOG2_E
        for n in range(per):
            proj_turned[s + n] = turned[:, n * blk : (n + 1) * blk]
            score_src[s + n] = got[:, n * blk : (n + 1) * blk]
    proj_dst[...] = mm(x_dst_ref[...], weight_ref[...]).astype(BF16)
    stacked = jnp.concatenate(
        [stack_dst, stack_src, jnp.zeros((LANES - 6 * heads, width), F32)], axis=0
    ).astype(BF16)
    got = mm(proj_dst[...], stacked, 1, 1) * LOG2_E
    shift = [got] + [pltpu.roll(got, LANES - n * heads, 1) for n in range(1, 6)]
    score_d = shift[0] + shift[1] + shift[2]
    pre_self = score_d + (shift[3] + shift[4] + shift[5])
    for h in range(heads):
        score_wide[h] = jnp.broadcast_to(score_d[:, h : h + 1], (dest, LANES))
    load_grad.wait()
    for d in range(dest // blk):
        cotan_turned[d] = grad_ref[d * blk : (d + 1) * blk, :].T

    numer[...] = jnp.zeros_like(numer)
    denom[...] = jnp.zeros_like(denom)
    grad_source[...] = jnp.zeros_like(grad_source)
    grad_score_src[...] = jnp.zeros_like(grad_score_src)
    grad_score_dst[...] = jnp.zeros_like(grad_score_dst)

    low = (iota((1, LANES), 1) < head_dim).astype(F32).astype(BF16)
    high = (iota((1, LANES), 1) >= head_dim).astype(F32).astype(BF16)
    second = iota((2 * blk, LANES), 0) // blk
    lane = iota((2 * blk, LANES), 1)

    def both(values):
        return jnp.concatenate([values * low, values * high], axis=0)

    ones_pair = [jnp.where(lane == 2 * g + second, 1.0, 0.0).astype(BF16) for g in range(pairs)]
    column = iota((LANES, 2 * blk), 0)
    column_head = iota((LANES, 2 * blk), 1) // blk
    minus_pair = [
        jnp.where(lax.rem(column, heads) == 2 * g + column_head, -1.0, 0.0) for g in range(pairs)
    ]
    minus_pair = [jnp.where(column < 2 * heads, m, 0.0).astype(BF16) for m in minus_pair]

    def forward(b, carry):
        r = pl.ds(pl.multiple_of(rows_ref[b] * blk, blk), blk)
        c = cols_ref[b]
        src = pl.ds(pl.multiple_of(c * blk, blk), blk)
        live = masks_ref[b] > 0
        scores = score_src[c]
        for g in range(pairs):
            at = slice(g * LANES, (g + 1) * LANES)
            found = []
            for h in (2 * g, 2 * g + 1):
                edge, slope = edge_terms(score_wide[h, r, :] + scores[h : h + 1, :])
                edge = jnp.where(live, edge, 0.0)
                weights[b, h] = edge
                slopes[b, h] = slope
                found.append(edge.astype(BF16))
            right = jnp.concatenate(
                [both(proj_src[src, at]), ones_pair[g]], axis=1
            )
            got = mm(jnp.concatenate(found, axis=1), right)
            numer[r, at] += got[:, :LANES]
            denom[r, :] += got[:, LANES:]
        return carry

    load_masks.wait()
    lax.fori_loop(0, count, forward, 0)

    lanes = iota((dest, LANES), 1)

    def two_pieces(values):
        top = values.astype(BF16).astype(F32)
        return (top + pltpu.roll(values - top, heads, 1)).astype(BF16)

    def over_heads(values):
        return jnp.where(lanes < heads, values, 0.0)

    feats = proj_dst[...].astype(F32)
    cotan = grad_ref[...].astype(F32)
    self_weight, self_slope = edge_terms(pre_self)
    self_weight = over_heads(self_weight)
    inverse = 1.0 / (denom[...] + jnp.where(lanes < heads, self_weight, 1.0))
    total = numer[...] + mm(two_pieces(self_weight), ones_heads) * feats
    attended = total * mm(two_pieces(over_heads(inverse)), ones_heads)
    narrow = over_heads(mm_split(cotan * attended, ones_turned, 2))
    centre[...] = two_pieces(narrow)
    self_att = self_weight * inverse
    self_pair = mm_split(cotan * feats, ones_turned, 2)
    self_grad = self_att * (self_pair - narrow) * self_slope
    for h in range(heads):
        inv_wide[h] = jnp.broadcast_to(inverse[:, h : h + 1], (dest, LANES))

    def backward(b, carry):
        d = rows_ref[b]
        r = pl.ds(pl.multiple_of(d * blk, blk), blk)
        c = cols_ref[b]
        nothing = jnp.zeros((head_dim, blk), BF16)
        for g in range(pairs):
            at = slice(g * LANES, (g + 1) * LANES)
            left = jnp.concatenate([grad_ref[r, at], centre[r, :]], axis=1)
            feats_turned = proj_turned[c, at, :]
            right = jnp.concatenate(
                [
                    jnp.concatenate([feats_turned[:head_dim], nothing], axis=1),
                    jnp.concatenate([nothing, feats_turned[head_dim:]], axis=1),
                    minus_pair[g],
                ],
                axis=0,
            )
            apart = mm(left, right)
            shares, sums = [], []
            for q in range(2):
                h = 2 * g + q
                share = weights[b, h] * inv_wide[h, r, :]
                grad = share * apart[:, q * blk : (q + 1) * blk] * slopes[b, h]
                sums.append(jnp.sum(grad, axis=0, keepdims=True))
                grad_score_dst[h, r, :] += grad
                shares.append(share.astype(BF16))
            grad_score_src[c, 2 * g : 2 * g + 2, :] += jnp.concatenate(sums, axis=0)
            got = mm(cotan_turned[d, at, :], jnp.concatenate(shares, axis=1))
            grad_source[c, at, :] += jnp.concatenate(
                [got[:head_dim, :blk], got[head_dim:, blk:]], axis=0
            )
        return carry

    lax.fori_loop(0, count, backward, 0)

    score_grad = self_grad
    for h in range(heads):
        score_grad += jnp.where(lanes == h, jnp.sum(grad_score_dst[h], axis=1, keepdims=True), 0.0)
    grads = (self_grad + pltpu.roll(score_grad, heads, 1)).astype(BF16)
    flat = (mm(two_pieces(self_att), ones_heads) * cotan + mm(grads, tall)).astype(BF16)
    grad_dst_ref[...] = mm(flat, weight_ref[...], 1, 1)
    part_weight = mm(x_dst_ref[...], flat, 0, 0)
    att_part = mm(grads, proj_dst[...], 0, 0)

    scores = jnp.concatenate([grad_score_src[s] for s in range(source_blocks)], axis=1).astype(BF16)
    spread_turned = spread_src.T.astype(BF16)
    for s in range(source_blocks):
        at = slice(s * blk, (s + 1) * blk)
        source[:, at] = (grad_source[s] + mm(spread_turned, scores[:, at])).astype(BF16)
    weight_turned_part = mm(source[...], x_all_ref[...])
    att_src_part = att_part[:heads] + mm(scores, proj_src[...])
    att_dst_part = att_part[heads : 2 * heads]
    for s in range(0, source_blocks, per):
        product = mm(weight_ref[...], source[:, s * blk : (s + per) * blk])
        for n in range(s, s + per):
            block = product[:, (n - s) * blk : (n - s + 1) * blk].T.astype(part_ref.dtype)
            for rep in range(reps):
                part_ref[n % 2, n // 2 * reps + rep, :share, :] = block[rep * share : (rep + 1) * share]
    part_weight += weight_turned_part.T
    tiles = [
        part_weight[n : n + CHUNK, g * LANES : (g + 1) * LANES].astype(part_ref.dtype)
        for g in range(pairs)
        for n in range(0, inputs, CHUNK)
    ]
    half = len(tiles) // 2
    for core in range(2):
        for owner in range(owners):
            part_ref[core, owner, share:, :] = (
                tiles[core * half + owner] if owner < half else jnp.zeros((CHUNK, LANES), part_ref.dtype)
            )
    src_row = jnp.sum(jnp.where(own, att_src_part, 0.0), axis=0, keepdims=True)
    dst_row = jnp.sum(jnp.where(own, att_dst_part, 0.0), axis=0, keepdims=True)
    stack = [row[:, g * LANES : (g + 1) * LANES] for row in (src_row, dst_row) for g in range(pairs)]
    att = jnp.concatenate(stack, axis=0)
    part_att_ref[...] = jnp.concatenate(
        [att.astype(BF16).astype(F32), att - att.astype(BF16).astype(F32)], axis=0
    ).astype(part_att_ref.dtype)


def place():
    panel, rep = lax.axis_index("panel"), lax.axis_index("rep")
    return panel // 2, panel % 2, rep, lax.axis_size("panel") // 2, lax.axis_size("rep")


def remote(src, dst, send, recv, panel, rep):
    return pltpu.make_async_remote_copy(
        src_ref=src, dst_ref=dst, send_sem=send, recv_sem=recv, device_id=(panel, rep), device_id_type=MESH
    )


def each(start, stop, step):
    def body(k, carry):
        step(k)
        return carry

    lax.fori_loop(start, stop, body, 0)


def gather_kernel(x_ref, out_ref, send, recv, pass_send, pass_recv):
    plane, core, rep, planes, _ = place()
    me = plane * 2 + core
    mate = plane * 2 + 1 - core
    barrier = pltpu.get_barrier_semaphore()

    def peer(k):
        return lax.rem(plane + k, planes) * 2 + core

    def greet(k):
        pl.semaphore_signal(barrier, inc=1, device_id=(peer(k), rep), device_id_type=MESH)

    each(1, planes, greet)
    pl.semaphore_signal(barrier, inc=1, device_id=(mate, rep), device_id_type=MESH)
    pl.semaphore_wait(barrier, planes)

    def own(k):
        return remote(x_ref, out_ref.at[me], send.at[k], recv.at[k], peer(k), rep)

    def passed(k):
        slot = lax.rem(plane + planes - k, planes) * 2 + core
        return remote(out_ref.at[slot], out_ref.at[slot], pass_send.at[k], pass_recv.at[k], mate, rep)

    each(1, planes, lambda k: own(k).start())
    first = remote(x_ref, out_ref.at[me], pass_send.at[0], pass_recv.at[0], mate, rep)
    first.start()
    out_ref[me] = x_ref[...]

    def hand_on(k):
        own(k).wait_recv()
        passed(k).start()

    each(1, planes, hand_on)
    first.wait()

    def finish(k):
        own(k).wait_send()
        passed(k).wait()

    each(1, planes, finish)


def gather(x_src):
    panels = lax.axis_size("panel")
    sems = pltpu.SemaphoreType.DMA((panels // 2,))
    vmem = pl.BlockSpec(memory_space=pltpu.VMEM)
    out = pl.pallas_call(
        gather_kernel,
        out_shape=jax.ShapeDtypeStruct((panels,) + x_src.shape, x_src.dtype),
        in_specs=[vmem],
        out_specs=vmem,
        scratch_shapes=[sems] * 4,
        compiler_params=pltpu.CompilerParams(collective_id=0, has_side_effects=True),
    )(x_src)
    return out.reshape(panels * x_src.shape[0], x_src.shape[1])


def reduce_kernel(
    part_hbm, att_hbm, rows_ref, chunks, att_out_ref,
    part_ref, att_ref, load_sems, mate_part, mate_att, merged, landed, chunk, tail, att_landed, mate_sems, swap_send, swap_recv,
    send, recv, row_send, row_recv, chunk_send, chunk_recv, att_send, att_recv, sum_send, sum_recv,
):
    plane, core, rep, planes, reps = place()
    owners, rows = merged.shape[:2]
    share = rows - CHUNK
    devices = 2 * owners
    me = plane * reps + rep
    panel = plane * 2 + core
    mate = plane * 2 + 1 - core
    index = panel * reps + rep
    load_part = pltpu.make_async_copy(part_hbm.at[core], part_ref, load_sems.at[0])
    load_att = pltpu.make_async_copy(att_hbm, att_ref, load_sems.at[1])
    load_part.start()
    load_att.start()
    barrier = pltpu.get_barrier_semaphore()

    def other(k):
        e = lax.rem(index + k, devices)
        return e // reps, lax.rem(e, reps)

    def greet(k):
        pl.semaphore_signal(barrier, inc=1, device_id=other(k), device_id_type=MESH)

    each(1, devices, greet)
    pl.semaphore_wait(barrier, devices - 1)

    pieces = swap_send.shape[0]
    span = owners // pieces

    def piece_at(n):
        return lax.rem(me // span + 1 + n, pieces)

    def swap(n):
        n = piece_at(n)
        piece = pl.ds(n * span, span)
        return remote(
            part_hbm.at[1 - core, piece], mate_part.at[piece], swap_send.at[n], swap_recv.at[n], mate, rep
        )

    swap_att = remote(att_hbm, mate_att, mate_sems.at[0], mate_sems.at[1], mate, rep)
    each(0, pieces, lambda n: swap(n).start())
    swap_att.start()

    def to_owner(d):
        slot = lax.rem(me - d + owners, owners)
        return remote(
            merged.at[d], landed.at[slot], send.at[d], recv.at[slot], d // reps * 2 + core, lax.rem(d, reps)
        )

    def from_owner(k):
        return remote(merged.at[0], landed.at[k], send.at[0], recv.at[k], mate, rep)

    def merge_piece(n):
        swap(n).wait_recv()

        def merge_send(j):
            d = piece_at(n) * span + lax.rem(me + j, span)
            summed = part_ref[d].astype(F32) + mate_part[d].astype(F32)
            merged[d] = summed.astype(BF16)

            @pl.when(d != me)
            def _():
                to_owner(d).start()

        each(0, span, merge_send)

    load_part.wait()
    each(0, pieces, merge_piece)

    swap_att.wait()
    load_att.wait()
    pair_att = att_ref[...].astype(F32) + mate_att[...].astype(F32)

    def as_pieces(pair):
        folded = pair[: CHUNK // 2] + pair[CHUNK // 2 :]
        top = folded.astype(BF16).astype(F32)
        return jnp.concatenate([top, folded - top], axis=0)

    tail[...] = as_pieces(pair_att).astype(BF16)

    def att_to_first(k):
        return remote(tail, att_landed.at[k], att_send.at[0], att_recv.at[k], core, 0)

    @pl.when(me != 0)
    def _():
        att_to_first(me).start()

    def collect(k, total):
        from_owner(k).wait_recv()
        return total + landed[k].astype(F32)

    total = lax.fori_loop(1, owners, collect, merged[me].astype(F32))

    chunk[...] = total[share:].astype(BF16)

    def spread(k):
        e_panel, e_rep = other(k)
        return remote(chunk, chunks.at[index], chunk_send.at[k], chunk_recv.at[k], e_panel, e_rep)

    def rows_to(k):
        part = rows_ref.at[pl.ds(pl.multiple_of(rep * share, share), share)]
        return remote(part, part, row_send.at[k], row_recv.at[k], panel, lax.rem(rep + k, reps))

    rows_ref[pl.ds(pl.multiple_of(rep * share, share), share), :] = total[:share]
    each(1, devices, lambda k: spread(k).start())
    each(1, reps, lambda k: rows_to(k).start())
    chunks[index] = chunk[...]

    def sum_to(k):
        return remote(
            att_out_ref, att_out_ref, sum_send.at[k], sum_recv.at[0], k // reps * 2 + core, lax.rem(k, reps)
        )

    @pl.when(me == 0)
    def _():
        def add_att(k, found):
            att_to_first(k).wait_recv()
            return found + att_landed[k].astype(F32)

        found = lax.fori_loop(1, owners, add_att, tail[...].astype(F32))
        att_out_ref[...] = as_pieces(found).astype(BF16)
        each(1, owners, lambda k: sum_to(k).start())
        each(1, owners, lambda k: sum_to(k).wait_send())

    @pl.when(me != 0)
    def _():
        att_to_first(me).wait_send()
        sum_to(me).wait_recv()

    each(0, pieces, lambda n: swap(n).wait_send())

    def sent(d):
        @pl.when(d != me)
        def _():
            to_owner(d).wait_send()

    each(0, owners, sent)
    each(1, devices, lambda k: spread(k).wait())
    each(1, reps, lambda k: rows_to(k).wait())


def unpack_kernel(reps, rows_ref, chunks, att_ref, grad_src_ref, grad_weight_ref, att_src_ref, att_dst_ref):
    grad_src_ref[...] = rows_ref[...]
    att = att_ref[...].astype(F32)
    att = att[: CHUNK // 2] + att[CHUNK // 2 :]
    heads, head_dim = att_src_ref.shape
    per = LANES // head_dim
    lines = [
        att[r : r + 1, q * head_dim : (q + 1) * head_dim] for r in range(2 * heads // per) for q in range(per)
    ]
    att_src_ref[...] = jnp.concatenate(lines[:heads], axis=0)
    att_dst_ref[...] = jnp.concatenate(lines[heads:], axis=0)
    inputs, width = grad_weight_ref.shape
    half = inputs * width // LANES // CHUNK // 2
    for n in range(2 * half):
        c, d = n // half, n % half
        sender = (d // reps * 2 + c) * reps + d % reps
        at, col = n * CHUNK % inputs, n * CHUNK // inputs * LANES
        grad_weight_ref[at : at + CHUNK, col : col + LANES] = chunks[sender].astype(F32)


def reduce(part, part_att, inputs, width, heads, rows):
    owners, lines = part.shape[1:3]
    reps = lax.axis_size("rep")
    pieces = 4
    vmem = pl.BlockSpec(memory_space=pltpu.VMEM)
    dma = pltpu.SemaphoreType.DMA
    packed = pl.pallas_call(
        reduce_kernel,
        out_shape=(
            jax.ShapeDtypeStruct((rows, inputs), F32),
            jax.ShapeDtypeStruct((2 * owners, CHUNK, LANES), BF16),
            jax.ShapeDtypeStruct((CHUNK, LANES), BF16),
        ),
        in_specs=[pl.BlockSpec(memory_space=pl.ANY)] * 2,
        out_specs=(vmem,) * 3,
        scratch_shapes=[
            pltpu.VMEM((owners, lines, LANES), BF16),
            pltpu.VMEM((CHUNK, LANES), BF16),
            dma((2,)),
            pltpu.VMEM((owners, lines, LANES), BF16),
            pltpu.VMEM((CHUNK, LANES), BF16),
            pltpu.VMEM((owners, lines, LANES), BF16),
            pltpu.VMEM((owners, lines, LANES), BF16),
            pltpu.VMEM((CHUNK, LANES), BF16),
            pltpu.VMEM((CHUNK, LANES), BF16),
            pltpu.VMEM((owners, CHUNK, LANES), BF16),
            dma((2,)),
            dma((pieces,)),
            dma((pieces,)),
            dma((owners,)),
            dma((owners,)),
            dma((reps,)),
            dma((reps,)),
            dma((2 * owners,)),
            dma((2 * owners,)),
            dma((1,)),
            dma((owners,)),
            dma((owners,)),
            dma((1,)),
        ],
        compiler_params=pltpu.CompilerParams(
            collective_id=1, has_side_effects=True, vmem_limit_bytes=62 * 1024 * 1024
        ),
    )(part, part_att)
    return pl.pallas_call(
        functools.partial(unpack_kernel, reps),
        out_shape=(
            jax.ShapeDtypeStruct((rows, inputs), F32),
            jax.ShapeDtypeStruct((inputs, width), F32),
            jax.ShapeDtypeStruct((heads, width // heads), F32),
            jax.ShapeDtypeStruct((heads, width // heads), F32),
        ),
        in_specs=[vmem] * 3,
        out_specs=(vmem,) * 4,
        compiler_params=pltpu.CompilerParams(vmem_limit_bytes=62 * 1024 * 1024),
    )(*packed)


def layer(x_all, x_dst, weight, att_src, att_dst, grad_out, rows, cols, masks, counts):
    heads = att_src.shape[0]
    inputs, width = weight.shape
    slots, blk = masks.shape[:2]
    sources, dest = x_all.shape[0], x_dst.shape[0]
    blocks = sources // blk
    reps = lax.axis_size("rep")
    owners = blocks // 2 * reps
    vmem = pl.BlockSpec(memory_space=pltpu.VMEM)
    smem = pl.BlockSpec(memory_space=pltpu.SMEM)
    return pl.pallas_call(
        layer_kernel,
        out_shape=(
            jax.ShapeDtypeStruct((dest, inputs), F32),
            jax.ShapeDtypeStruct((2, owners, blk // reps + CHUNK, LANES), BF16),
            jax.ShapeDtypeStruct((CHUNK, LANES), BF16),
        ),
        in_specs=[smem] * 3 + [vmem] * 5 + [pl.BlockSpec(memory_space=pl.ANY)] * 2,
        out_specs=(vmem,) * 3,
        scratch_shapes=[
            pltpu.VMEM((sources, width), BF16),
            pltpu.VMEM((blocks, width, blk), BF16),
            pltpu.VMEM((dest, width), BF16),
            pltpu.VMEM((dest // blk, width, blk), BF16),
            pltpu.VMEM((blocks, heads, blk), F32),
            pltpu.VMEM((heads, dest, LANES), F32),
            pltpu.VMEM((heads, dest, LANES), F32),
            pltpu.VMEM((slots, heads, blk, blk), F32),
            pltpu.VMEM((slots, heads, blk, blk), F32),
            pltpu.VMEM((dest, width), F32),
            pltpu.VMEM((dest, LANES), F32),
            pltpu.VMEM((dest, LANES), BF16),
            pltpu.VMEM((blocks, width, blk), F32),
            pltpu.VMEM((blocks, heads, blk), F32),
            pltpu.VMEM((heads, dest, LANES), F32),
            pltpu.VMEM((width, sources), BF16),
            pltpu.VMEM(grad_out.shape, grad_out.dtype),
            pltpu.VMEM(masks.shape, masks.dtype),
            pltpu.SemaphoreType.DMA((2,)),
        ],
        compiler_params=pltpu.CompilerParams(vmem_limit_bytes=62 * 1024 * 1024),
    )(rows, cols, counts, x_all, x_dst, weight, att_src, att_dst, grad_out, masks)


def shards(
    x_src, x_dst, weight, att_src, att_dst, grad_out, block_rows, block_cols, block_masks, block_counts
):
    x_all = gather(x_src)
    grad_dst, part, part_att = layer(
        x_all, x_dst, weight, att_src, att_dst, grad_out, block_rows, block_cols, block_masks, block_counts
    )
    grad_src, grad_weight, grad_att_src, grad_att_dst = reduce(
        part, part_att, weight.shape[0], weight.shape[1], att_src.shape[0], x_src.shape[0]
    )
    return grad_src, grad_dst, grad_weight, grad_att_src, grad_att_dst


def solution(mesh):
    both = P(("panel", "rep"))
    return jax.shard_map(
        shards,
        mesh=mesh,
        in_specs=(P("panel", None), both, P(), P(), P(), both, both, both, both, both),
        out_specs=(P("panel", None), both, P(), P(), P()),
        check_vma=False,
    )
```
